256 devices in a mesh: gx: 16 (over z, core), gy: 16 (over y, x).
Axes of the slice: x: 4, y: 4, z: 8, core: 2. Of those that a mesh axis runs over, the one named last changes fastest.
Arguments:
- pressure: float32 [32, 512, 2048], P(None, 'gx', 'gy'), may hold values from -4 to 4
- ksat: float32 [32, 512, 2048], P(None, 'gx', 'gy'), may hold values from 0.2 to 2
- age_mean: float32 [32, 512, 2048], P(None, 'gx', 'gy'), may hold values from 1 to 10
- age_var: float32 [32, 512, 2048], P(None, 'gx', 'gy'), may hold values from 0.5 to 5
- remap: int32 [512, 16], P('gx', 'gy'), may hold values from 0 to 511, as said below
- forcing: float32 [7, 512, 2048], P(None, 'gx', 'gy'), may hold values from 0 to 1.5
- land_state: float32 [2, 512, 2048], P(None, 'gx', 'gy'), may hold values from 0 to 1
- veg_class: int32 [512, 2048], P('gx', 'gy'), may hold values from 0 to 16
- veg_table: float32 [5, 17], replicated, may hold values from 0.3 to 0.9
Outputs:
- pressure_next: float32 [32, 512, 2048], P(None, 'gx', 'gy')
- age_mean_next: float32 [32, 512, 2048], P(None, 'gx', 'gy')
- age_var_next: float32 [32, 512, 2048], P(None, 'gx', 'gy')
- land_next: float32 [2, 512, 2048], P(None, 'gx', 'gy')
The draws below stay inside these ranges and needn't reach their ends.
Inputs may be any that keep to these rules, and one draw needn't show every extreme that they name: `remap`: each entry is d * 32 + s: the tile is handled by slot s of the device at index d along gy with the same gx index; within each gx index every slot receives exactly one tile. A device hands 0, 2 or 4 tiles to each device along gy, and in every draw some device hands 4 tiles to some device.
All inputs are finite; a program needn't handle non-finite values.
Results may differ from the reference program's by a relative error of at most 0.0003.
Values sent between devices are 32-bit elements; how exact they have to be, the bound alone decides.
A program may use at most 64 MiB of HBM per device.

```python
import math
import jax
import jax.numpy as jnp

CX = 32
CY = 128
NZ = 32
NROOT = 2
FORC = 7
NVEG = 17
NX = 512
NY = 2048
N_GX = 16
N_GY = 16


def draw_remap(key, part):
    key = jax.random.fold_in(key, 7)
    per_peer = CX // N_GY

    def one_group(group_key):
        order_key, shuffle_key = jax.random.split(group_key)
        chosen = jax.random.permutation(order_key, N_GY)
        shifted = jnp.roll(chosen, -1)
        target = jnp.arange(N_GY)
        counts = per_peer * (1 + (target[None, :] == chosen[:, None]).astype(jnp.int32) - (target[None, :] == shifted[:, None]).astype(jnp.int32))
        bounds = jnp.cumsum(counts, axis=1)
        starts = bounds - counts
        row_ids = jnp.arange(CX)
        target_dev = jnp.sum((row_ids[None, :, None] >= bounds[:, None, :]).astype(jnp.int32), axis=2)
        target_hot = (target_dev[:, :, None] == target[None, None, :]).astype(jnp.int32)
        position = row_ids[None, :] - jnp.sum(target_hot * starts[:, None, :], axis=2)
        earlier = jnp.cumsum(counts, axis=0) - counts
        slot_ids = jnp.sum(target_hot * earlier[:, None, :], axis=2) + position
        coded = target_dev * CX + slot_ids

        def shuffle_one(row_key):
            return jax.random.permutation(row_key, CX)
        shuffles = jax.vmap(shuffle_one)(jax.random.split(shuffle_key, N_GY))
        coded = jnp.take_along_axis(coded, shuffles, axis=1)
        return coded.T
    groups = jax.vmap(one_group)(jax.random.split(key, N_GX))
    return groups.reshape(N_GX * CX, N_GY).astype(jnp.int32)


def touch_ends(drawn, key, smallest, largest):
    place = [jax.random.randint(jax.random.fold_in(key, axis), (), 0, length) for axis, length in enumerate(drawn.shape)]
    main_axis = drawn.shape.index(max(drawn.shape))
    next_to = place[:main_axis] + [(place[main_axis] + 1) % drawn.shape[main_axis]] + place[main_axis + 1:]
    return drawn.at[tuple(place)].set(smallest).at[tuple(next_to)].set(largest)


def block_levels(stream_key, extent, cuts, low, high):
    gain = 1.0
    for axis_at, shards_of in cuts:
        heights = jax.random.uniform(jax.random.fold_in(jax.random.fold_in(stream_key, 6), axis_at), (shards_of,), jnp.float32, low / len(cuts), high / len(cuts))
        gain = gain * jnp.repeat(jnp.exp(heights), extent[axis_at] // shards_of).reshape((-1,) + (1,) * (len(extent) - 1 - axis_at))
    return gain


def bell_draw(own_key, extent, scale, bound, cuts=(), held_as=jnp.bfloat16):
    factor_of = block_levels(own_key, extent, cuts, -0.22, 0.18) if cuts else 1.0
    values = jax.random.normal(own_key, extent, jnp.float32) * scale * factor_of
    return jnp.minimum(jnp.maximum(values, -bound), bound).astype(held_as)


def setup_inputs(seed: int = 0) -> dict:
    streams_of = jax.random.split(jax.random.key(seed), 10)
    return {
        "pressure": bell_draw(streams_of[0], (NZ, NX, NY), 1.0, 4.0, ((1, 16), (2, 16)), jnp.float32),
        "ksat": jnp.clip(jnp.exp(math.log(2.0) - 2.3025851 * jax.random.uniform(streams_of[1], (NZ, NX, NY), jnp.float32) ** block_levels(streams_of[1], (NZ, NX, NY), ((1, 16), (2, 16)), -0.2, 0.2)), 0.2, 2.0),
        "age_mean": jnp.clip(jnp.exp(math.log(10.0) - 2.3025851 * jax.random.uniform(streams_of[2], (NZ, NX, NY), jnp.float32) ** block_levels(streams_of[2], (NZ, NX, NY), ((1, 16), (2, 16)), -0.2, 0.2)), 1.0, 10.0),
        "age_var": jnp.clip(jnp.exp(math.log(5.0) - 2.3025851 * jax.random.uniform(streams_of[3], (NZ, NX, NY), jnp.float32) ** block_levels(streams_of[3], (NZ, NX, NY), ((1, 16), (2, 16)), -0.2, 0.2)), 0.5, 5.0),
        "remap": draw_remap(jax.random.fold_in(streams_of[9], 71), 0),
        "forcing": jnp.clip(1.5 * jax.random.uniform(streams_of[5], (FORC, NX, NY), jnp.float32) ** block_levels(streams_of[5], (FORC, NX, NY), ((1, 16), (2, 16)), -0.2, 0.2), 0.0, 1.5),
        "land_state": jnp.clip(1.0 * jax.random.uniform(streams_of[6], (2, NX, NY), jnp.float32) ** block_levels(streams_of[6], (2, NX, NY), ((1, 16), (2, 16)), -0.2, 0.2), 0.0, 1.0),
        "veg_class": touch_ends(jax.random.randint(streams_of[7], (NX, NY), 0, NVEG), jax.random.fold_in(streams_of[7], 1), 0, NVEG - 1).astype(jnp.int32),
        "veg_table": jnp.clip(jax.random.uniform(streams_of[8], (5, NVEG), jnp.float32, 0.3, 0.9), 0.3, 0.9),
    }


step_time = 0.2
side_weight = 0.5

def water_content(head_field):
    return 0.05 + 0.4 * jax.nn.sigmoid(head_field)

def conductance(head_field, ksat_field):
    wetness = jax.nn.sigmoid(head_field)
    return ksat_field * (0.05 + wetness * wetness)

def vertical_net(vertical_q, template):
    zero_layer = jnp.zeros_like(template[:1])
    return jnp.concatenate([vertical_q, zero_layer], 0) - jnp.concatenate([zero_layer, vertical_q], 0)

def layer_sources(sources, template):
    roots = sources.shape[0] - 1
    rest = jnp.zeros_like(template[roots:])
    extraction = jnp.concatenate([sources[1:], rest], 0)
    inflow = jnp.concatenate([sources[:1], jnp.zeros_like(template[1:])], 0)
    return (extraction, inflow)

def neighbour_parts():
    return [(slice(None, -2), slice(1, -1)), (slice(2, None), slice(1, -1)), (slice(1, -1), slice(None, -2)), (slice(1, -1), slice(2, None))]

def thomas(lower, diagonal, upper, right):
    layers = diagonal.shape[0]
    ratios = [upper[0] / diagonal[0]]
    values = [right[0] / diagonal[0]]
    for layer in range(1, layers):
        pivot = diagonal[layer] - lower[layer] * ratios[-1]
        ratios.append(upper[layer] / pivot)
        values.append((right[layer] - lower[layer] * values[-1]) / pivot)
    result = [values[-1]]
    for layer in range(layers - 2, -1, -1):
        result.append(values[layer] - ratios[layer] * result[-1])
    return jnp.stack(result[::-1], 0)

def newton_step(head_ext, ksat_ext, head_old, sources):
    centre = head_ext[:, 1:-1, 1:-1]
    conduct_all = conductance(head_ext, ksat_ext)
    conduct_mid = conduct_all[:, 1:-1, 1:-1]
    side_out = jnp.zeros_like(centre)
    side_diag = jnp.zeros_like(centre)
    for row_part, col_part in neighbour_parts():
        face_k = side_weight * jnp.sqrt(conduct_mid * conduct_all[:, row_part, col_part])
        side_out = side_out + face_k * (centre - head_ext[:, row_part, col_part])
        side_diag = side_diag + face_k
    vertical_k = jnp.sqrt(conduct_mid[:-1] * conduct_mid[1:])
    vertical_q = vertical_k * (centre[:-1] - centre[1:] + 1.0)
    extraction, inflow = layer_sources(sources, centre)
    residual = (water_content(centre) - water_content(head_old)) / step_time + side_out + vertical_net(vertical_q, centre) + extraction - inflow
    wetness = jax.nn.sigmoid(centre)
    zero_layer = jnp.zeros_like(centre[:1])
    k_below = jnp.concatenate([vertical_k, zero_layer], 0)
    k_above = jnp.concatenate([zero_layer, vertical_k], 0)
    diagonal = 0.4 * wetness * (1.0 - wetness) / step_time + side_diag + k_below + k_above
    update = thomas(-k_above, diagonal, -k_below, -residual)
    return centre + update

def age_step(head_ext, ksat_ext, age_ext, mom_ext, head_old, sources):
    centre = head_ext[:, 1:-1, 1:-1]
    conduct_all = conductance(head_ext, ksat_ext)
    conduct_mid = conduct_all[:, 1:-1, 1:-1]
    age_mid = age_ext[:, 1:-1, 1:-1]
    mom_mid = mom_ext[:, 1:-1, 1:-1]
    age_out = jnp.zeros_like(centre)
    mom_out = jnp.zeros_like(centre)
    for row_part, col_part in neighbour_parts():
        side_q = side_weight * jnp.sqrt(conduct_mid * conduct_all[:, row_part, col_part]) * (centre - head_ext[:, row_part, col_part])
        flow_out = jnp.maximum(side_q, 0.0)
        flow_in = jnp.minimum(side_q, 0.0)
        age_out = age_out + flow_out * age_mid + flow_in * age_ext[:, row_part, col_part]
        mom_out = mom_out + flow_out * mom_mid + flow_in * mom_ext[:, row_part, col_part]
    vertical_k = jnp.sqrt(conduct_mid[:-1] * conduct_mid[1:])
    vertical_q = vertical_k * (centre[:-1] - centre[1:] + 1.0)
    down_plus = jnp.maximum(vertical_q, 0.0)
    down_minus = jnp.minimum(vertical_q, 0.0)
    age_down = down_plus * age_mid[:-1] + down_minus * age_mid[1:]
    mom_down = down_plus * mom_mid[:-1] + down_minus * mom_mid[1:]
    extraction, inflow = layer_sources(sources, centre)
    water_old = water_content(head_old)
    water_new = water_content(centre)
    age_next = (water_old * age_mid - step_time * (age_out + vertical_net(age_down, centre) + extraction * age_mid) + step_time * water_new) / water_new
    mom_next = (water_old * mom_mid - step_time * (mom_out + vertical_net(mom_down, centre) + extraction * mom_mid) + 2.0 * step_time * water_new * age_next) / water_new
    return (age_next, mom_next - age_next * age_next)

def land_step(land_top, forcing, land_state, veg_class, veg_table):
    veg_count = veg_table.shape[1]
    veg_params = jnp.zeros((veg_table.shape[0],) + veg_class.shape, forcing.dtype)
    for veg_id in range(veg_count):
        veg_params = veg_params + jnp.where(veg_class == veg_id, 1.0, 0.0).astype(forcing.dtype)[None] * veg_table[:, veg_id][:, None, None]
    albedo, conduct, capacity, et_factor, root_decay = (veg_params[0], veg_params[1], veg_params[2], veg_params[3], veg_params[4])
    shortwave, longwave, air_temp, humidity = (forcing[0], forcing[1], forcing[2], forcing[3])
    wind_speed, surf_press, rainfall = (forcing[4], forcing[5], forcing[6])
    skin_temp, canopy = (land_state[0], land_state[1])
    roots = land_top.shape[0] - 1
    skin_next = (skin_temp + 0.5 * ((1.0 - albedo) * 2.0 * shortwave + 0.5 * longwave + air_temp)) / 1.5
    demand = conduct * jax.nn.softplus(skin_next) * (1.0 + wind_speed) * (1.0 - 0.5 * humidity) / (0.5 + surf_press)
    root_scale = (1.0 - root_decay) / (1.0 - root_decay ** roots)
    extracts = [0.5 * et_factor * demand * root_scale * root_decay ** layer * jax.nn.sigmoid(land_top[layer]) for layer in range(roots)]
    wetted = canopy + rainfall
    dripping = jnp.maximum(wetted - capacity, 0.0)
    canopy_next = (wetted - dripping) * capacity / (demand + capacity)
    throughfall = dripping + 0.5 * rainfall
    infil_limit = land_top[roots] * (1.0 + 2.0 * (1.0 - jax.nn.sigmoid(land_top[0])))
    infiltration = infil_limit * throughfall / (infil_limit + throughfall)
    return (jnp.stack([infiltration] + extracts, 0), jnp.stack([skin_next, canopy_next], 0))

def to_land(fields, remap):
    count = fields.shape[0]
    tile_data = fields.reshape(count, N_GX, CX, N_GY, CY).transpose(1, 2, 3, 0, 4).reshape(N_GX, CX * N_GY, count, CY)
    coded = remap.reshape(N_GX, CX * N_GY).astype(jnp.int32)

    def placed(tiles_one, codes_one):
        return jnp.zeros_like(tiles_one).at[codes_one].set(tiles_one)
    landed = jax.vmap(placed)(tile_data, coded)
    return landed.reshape(N_GX, N_GY, CX, count, CY).transpose(3, 0, 2, 1, 4).reshape(count, NX, NY)

def to_soil(fields, remap):
    count = fields.shape[0]
    landed = fields.reshape(count, N_GX, CX, N_GY, CY).transpose(1, 3, 2, 0, 4).reshape(N_GX, N_GY * CX, count, CY)
    coded = remap.reshape(N_GX, CX * N_GY).astype(jnp.int32)

    def picked(land_one, codes_one):
        return land_one[codes_one]
    tile_data = jax.vmap(picked)(landed, coded)
    return tile_data.reshape(N_GX, CX, N_GY, count, CY).transpose(3, 0, 1, 2, 4).reshape(count, NX, NY)

def padded(field):
    return jnp.pad(field, ((0, 0), (1, 1), (1, 1)))

def reference(pressure, ksat, age_mean, age_var, remap, forcing, land_state, veg_class, veg_table):
    top_fields = jnp.concatenate([pressure[:NROOT], ksat[:1]], 0)
    land_top = to_land(top_fields, remap)
    land_fluxes, land_next = land_step(land_top, forcing, land_state, veg_class, veg_table)
    soil_fluxes = to_soil(land_fluxes, remap)
    moment = age_var + age_mean * age_mean
    ksat_ext = padded(ksat)
    current = pressure
    for newton_turn in range(2):
        current = newton_step(padded(current), ksat_ext, pressure, soil_fluxes)
    age_next, var_next = age_step(padded(current), ksat_ext, padded(age_mean), padded(moment), pressure, soil_fluxes)
    return (current, age_next, var_next, land_next)
```

```python
import functools
import math

import jax
import jax.numpy as jnp
from jax import lax
from jax.experimental import pallas as pl
from jax.experimental.pallas import tpu as pltpu
from jax.sharding import PartitionSpec as P

LANES = 128
HALF = 64
PAD = 8
SLOTS = 4
F32 = jnp.float32
BF16 = jnp.bfloat16
MESH = pl.DeviceIdType.MESH


def sigmoid(x):
    return 0.5 * jnp.tanh(0.5 * x) + 0.5


def root_conduct(s, ksat):
    x = ksat * (0.05 + s * s)
    return x * lax.rsqrt(x)


def iota(shape, dim):
    return lax.broadcasted_iota(jnp.int32, shape, dim)


def pieces(x):
    high = x.astype(BF16)
    rest = x - high.astype(F32)
    mid = rest.astype(BF16)
    return high, mid, (rest - mid.astype(F32)).astype(BF16)


def pick_rows(one_hot, x):
    n = x.shape[1]
    out = jnp.dot(one_hot.astype(BF16), jnp.concatenate(pieces(x), axis=1), preferred_element_type=F32)
    return (out[:, 2 * n:] + out[:, n:2 * n]) + out[:, :n]


def kernel(
    Z, X, GX, GY,
    p_hbm, k_hbm, a_hbm, v_hbm, remap_hbm, forc_hbm, state_hbm, veg_hbm, table_hbm,
    p_out, a_out, v_out, land_out,
    rp, wp, ap, mp, dg, rs, pc, ks, s0, sc, gg, yy, kvs, age, var, av, vv,
    remap, forc, state, veg, table, landn,
    osend, orecv, fsend, frecv,
    lsend, lrecv, usend, urecv, dsend, drecv,
    load_sem, out_sem, o_ssem, o_rsem, f_ssem, f_rsem, h_ssem, h_rsem,
):
    gx, gy = lax.axis_index("gx"), lax.axis_index("gy")
    up, down = lax.rem(gx + GX - 1, GX), lax.rem(gx + 1, GX)
    left, right = lax.rem(gy + GY - 1, GY), lax.rem(gy + 1, GY)
    stride = X + 2 * PAD
    side = math.isqrt(GY)

    def layer(k, shift=0):
        return pl.ds(pl.multiple_of(k * stride, 8) + (PAD + shift), X)

    def block(k):
        return pl.ds(pl.multiple_of(k * X, 8), X)

    def far(o):
        dy, dx = o // side, o % side
        return min(dy, side - dy) + min(dx, side - dx)

    offsets = sorted(range(1, GY), key=lambda o: -far(o))
    my_y, my_x = gy // side, lax.rem(gy, side)
    peers = {
        o: lax.rem(my_y + o // side, side) * side + lax.rem(my_x + o % side, side) for o in offsets
    }

    def load(src, dst, n):
        c = pltpu.make_async_copy(src, dst, load_sem.at[n])
        c.start()
        return c

    barrier = pltpu.get_barrier_semaphore()
    for o in offsets:
        pl.semaphore_signal(barrier, inc=1, device_id={"gy": peers[o]}, device_id_type=MESH)
    for d in (up, down):
        pl.semaphore_signal(barrier, inc=1, device_id={"gx": d}, device_id_type=MESH)
    c_remap = load(remap_hbm, remap, 0)
    c_forc = load(forc_hbm, forc, 3)
    c_state = load(state_hbm, state, 4)
    c_veg = load(veg_hbm, veg, 5)
    c_table = load(table_hbm, table, 6)
    c_p = load(p_hbm, pc, 1)
    c_k = load(k_hbm, ks, 2)
    c_a = load(a_hbm, age, 7)
    c_v = load(v_hbm, var, 8)

    def send(src, dst, ssem, rsem, where):
        c = pltpu.make_async_remote_copy(
            src_ref=src, dst_ref=dst, send_sem=ssem, recv_sem=rsem,
            device_id=where, device_id_type=MESH,
        )
        c.start()
        return c

    lane = iota((X, LANES), 1)
    pair = lane >> 1
    first_lane, last_lane = lane == 0, lane == LANES - 1
    edge = first_lane | last_lane
    even = (lane & 1) == 0
    zero = jnp.zeros((X, LANES), F32)
    pad = jnp.zeros((PAD, LANES), F32)

    c_remap.wait()
    bits = X.bit_length() - 1
    code_row = remap[...]
    eye = iota((X, X), 0) == iota((X, X), 1)
    code_col = jnp.sum(jnp.where(eye, jnp.broadcast_to(code_row, (X, X)), 0), axis=1, keepdims=True)
    dest_row, dest_col = code_row >> bits, code_col >> bits
    slot_col = code_col & (X - 1)
    same = jnp.broadcast_to(dest_col, (X, X)) == jnp.broadcast_to(dest_row, (X, X))
    rank_row = jnp.sum(jnp.where(same & (iota((X, X), 0) < iota((X, X), 1)), 1, 0), axis=0, keepdims=True)
    rank_col = jnp.sum(jnp.where(same & (iota((X, X), 1) < iota((X, X), 0)), 1, 0), axis=1, keepdims=True)
    rows = 8 * GY
    row_id = iota((rows, X), 0)
    row_key = (row_id >> 3) * SLOTS + (row_id & (SLOTS - 1))
    tile_of_row = (row_key == jnp.broadcast_to(dest_row * SLOTS + rank_row, (rows, X))).astype(BF16)
    slot_of_tile = (jnp.broadcast_to(slot_col, (X, LANES)) == iota((X, LANES), 1)).astype(BF16)
    osend[...] = jnp.dot(tile_of_row, slot_of_tile, preferred_element_type=F32).reshape(GY, 8, LANES)

    pl.semaphore_wait(barrier, GY + 1)

    sends = []
    o_copies = [
        send(osend.at[peers[o]], orecv.at[gy], o_ssem.at[o], o_rsem.at[o], {"gy": peers[o]}) for o in offsets
    ]
    sends += o_copies
    orecv[gy] = osend[gy]

    row_of_tile = jnp.broadcast_to(dest_col * 8 + rank_col, (X, rows))
    take = jnp.concatenate(
        [(row_of_tile + n == iota((X, rows), 1)).astype(F32) for n in (0, SLOTS)], axis=0
    )

    c_veg.wait()
    c_table.wait()
    c_forc.wait()
    c_state.wait()
    cls = veg[...]
    nveg = table.shape[1]
    par = [jnp.full((X, LANES), table[i, 0], F32) for i in range(5)]
    for v in range(1, nveg):
        hit = cls == v
        par = [jnp.where(hit, table[i, v], par[i]) for i in range(5)]
    albedo, conduct, capacity, et_factor, decay = par
    skin = (state[0] + 0.5 * ((1.0 - albedo) * 2.0 * forc[0] + 0.5 * forc[1] + forc[2])) / 1.5
    soft = jnp.maximum(skin, 0.0) + jnp.log(1.0 + jnp.exp(-jnp.abs(skin)))
    demand = conduct * soft * (1.0 + forc[4]) * (1.0 - 0.5 * forc[3]) / (0.5 + forc[5])
    wetted = state[1] + forc[6]
    drip = jnp.maximum(wetted - capacity, 0.0)
    canopy = (wetted - drip) * capacity / (demand + capacity)
    through = drip + 0.5 * forc[6]
    draw0 = 0.5 * et_factor * demand / (1.0 + decay)
    draw1 = draw0 * decay
    landn[0] = skin
    landn[1] = canopy
    c_land = pltpu.make_async_copy(landn, land_out, out_sem.at[0])
    c_land.start()
    fields = jnp.concatenate([draw0, draw1, through], axis=1)

    for ref in (rp, wp, ap, mp):
        for k in range(Z):
            ref[k * stride:k * stride + PAD, :] = pad
            ref[k * stride + PAD + X:(k + 1) * stride, :] = pad

    def edge_rows(k, n, value):
        usend[n, pl.ds(k, 1), :] = value[0:1]
        dsend[n, pl.ds(k, 1), :] = value[X - 1:X]

    def wet(k, turn):
        p = pc[k]
        s = sigmoid(p)
        r = root_conduct(s, ks[k])
        w = r * p
        (sc if turn else s0)[k] = s
        rp[layer(k), :] = r
        wp[layer(k), :] = w
        return p, s, r, w

    def near(ref, k, value):
        return (
            (ref[layer(k, -1), :] + ref[layer(k, 1), :])
            + jnp.where(first_lane, 0.0, pltpu.roll(value, 1, 1))
            + jnp.where(last_lane, 0.0, pltpu.roll(value, LANES - 1, 1))
        )

    def assemble(turn, k, c):
        p1, r1, kv1, qv1, diag1, res1 = c[:6]
        p, s, r, w = wet(k, turn)
        kv = r1 * r
        qv = kv * (p1 - p + 1.0)
        dg[block(k), :] = diag1 + kv1 + kv
        rs[block(k), :] = res1 + (qv - qv1)
        kvs[k] = kv
        sum1, sum2 = near(rp, k, r), near(wp, k, w)
        hr = 0.5 * r
        diag = 2.0 * s * (1.0 - s) + hr * sum1
        res = hr * (p * sum1 - sum2)
        if turn:
            res = res + 2.0 * (s - s0[k])
            return p, r, kv, qv, diag, res
        edge_rows(k, 0, p)
        edge_rows(k, 1, ks[k])
        acc = jnp.where(pair == k, pltpu.roll(p, 2 * k + 1, 1), c[6])
        acc = jnp.where(pair == k + HALF // 2, pltpu.roll(ks[k], HALF + 2 * k + 1, 1), acc)
        return p, r, kv, qv, diag, res, acc

    def finish(c):
        _, _, kv1, qv1, diag1, res1 = c[:6]
        dg[block(Z), :] = diag1 + kv1
        rs[block(Z), :] = res1 - qv1
        kvs[Z] = zero

    c_p.wait()
    c_k.wait()
    c = lax.fori_loop(0, Z, functools.partial(assemble, 0), (zero,) * 7, unroll=2)
    lsend[0] = c[6]
    finish(c)

    def halo(phase, row0, nrows):
        cs = [
            send(lsend.at[phase], lrecv.at[phase, 0], h_ssem.at[phase, 0], h_rsem.at[phase, 0], {"gy": right}),
            send(lsend.at[phase], lrecv.at[phase, 1], h_ssem.at[phase, 1], h_rsem.at[phase, 1], {"gy": left}),
            send(usend.at[pl.ds(row0, nrows)], urecv.at[pl.ds(row0, nrows)],
                 h_ssem.at[phase, 2], h_rsem.at[phase, 2], {"gx": up}),
            send(dsend.at[pl.ds(row0, nrows)], drecv.at[pl.ds(row0, nrows)],
                 h_ssem.at[phase, 3], h_rsem.at[phase, 3], {"gx": down}),
        ]
        sends.extend(cs)
        return cs

    h0 = halo(0, 0, 2)

    c_a.wait()
    c_v.wait()

    def moments(k, acc):
        a = age[k]
        m = var[k] + a * a
        ap[layer(k), :] = a
        mp[layer(k), :] = m
        edge_rows(k, 2, a)
        edge_rows(k, 3, m)
        acc = jnp.where(pair == k, pltpu.roll(a, 2 * k + 1, 1), acc)
        return jnp.where(pair == k + HALF // 2, pltpu.roll(m, HALF + 2 * k + 1, 1), acc)

    lsend[1] = lax.fori_loop(0, Z, moments, zero, unroll=2)
    h1 = halo(1, 2, 2)

    for c in o_copies:
        c.wait_recv()
    packed = pick_rows(orecv[...].reshape(rows, LANES)[:, :X], fields)
    low = (iota((rows, LANES), 0) & 7) < SLOTS
    first_half = jnp.where(low, packed[:, :LANES], packed[:, LANES:2 * LANES])
    fsend[:, 0:8, :] = first_half.reshape(GY, 8, LANES)
    fsend[:, 8:16, :] = packed[:, 2 * LANES:].reshape(GY, 8, LANES)
    f_copies = [
        send(fsend.at[peers[o]], frecv.at[gy], f_ssem.at[o], f_rsem.at[o], {"gy": peers[o]}) for o in offsets
    ]
    sends += f_copies
    frecv[gy] = fsend[gy]

    def lane_halo(phase):
        return jnp.where(
            even, pltpu.roll(lrecv[phase, 1], LANES - 1, 1), pltpu.roll(lrecv[phase, 0], 1, 1)
        )

    for c in h0:
        c.wait_recv()
    lane_pk = lane_halo(0)
    inside = jnp.where(even, jnp.where(gy < GY - 1, 1.0, 0.0), jnp.where(gy > 0, 1.0, 0.0))
    above_in = jnp.where(gx > 0, 1.0, 0.0)
    below_in = jnp.where(gx < GX - 1, 1.0, 0.0)

    def compact_k(packed):
        return jnp.where(lane < HALF, pltpu.roll(packed, HALF, 1), 1.0)

    edge_k = (
        (compact_k(lane_pk), compact_k(lsend[0]), inside),
        (drecv[1], usend[1], above_in),
        (urecv[1], dsend[1], below_in),
    )

    def edge_p(phase, n):
        return ((lane_halo(phase), lsend[phase]), (drecv[n], usend[n]), (urecv[n], dsend[n]))

    def edge_state(phase, n):
        out = []
        for (hk, ok, inner), (hp, op) in zip(edge_k, edge_p(phase, n)):
            hr = root_conduct(sigmoid(hp), hk) * inner
            out.append((hr, hr * hp, root_conduct(sigmoid(op), ok), op))
        return out

    def add_rows(ref, above, below):
        for row, value in ((0, above), (X - 1, below)):
            at = pl.ds(X + row, Z, stride=X)
            ref[at, :] = ref[at, :] + value

    def spread(k, compact):
        return jnp.where(edge, pltpu.roll(compact, LANES - 1 - 2 * k, 1), 0.0)

    def side_terms(phase, n):
        terms = [
            (0.5 * own_r * hr, 0.5 * own_r * (own_p * hr - hw)) for hr, hw, own_r, own_p in edge_state(phase, n)
        ]
        add_rows(dg, terms[1][0], terms[2][0])
        add_rows(rs, terms[1][1], terms[2][1])
        return terms[0]

    def eliminate(k, coupling, inv, b, lanes, source=None):
        diag = dg[block(k + 1), :] + spread(k, lanes[0])
        res = rs[block(k + 1), :] + spread(k, lanes[1])
        if source is not None:
            res = res + source
        g = coupling * inv
        b = g * b - res
        inv = 1.0 / (diag - coupling * g)
        yy[k] = b * inv
        return g, inv, b

    def from_below(lanes, k, c, source=None):
        g, inv, b = eliminate(k, kvs[k + 1], *c, lanes, source)
        gg[k + 1] = g
        return inv, b

    def update(k, n, d, acc):
        p = pc[k] + d
        pc[k] = p
        edge_rows(k, n, p)
        return jnp.where(pair == k, pltpu.roll(p, 2 * k + 1, 1), acc)

    lanes = side_terms(0, 0)
    c = lax.fori_loop(0, Z - 2, lambda i, c: from_below(lanes, Z - 1 - i, c), (zero, zero), unroll=2)
    for f in f_copies:
        f.wait_recv()
    got = pick_rows(
        take,
        jnp.concatenate(
            [frecv[:, 0:8, :].reshape(rows, LANES), frecv[:, 8:16, :].reshape(rows, LANES)], axis=1
        ),
    )
    ext0 = got[:X, :LANES] * s0[0]
    ext1 = got[X:, :LANES] * s0[1]
    fall = got[:X, LANES:]
    limit = ks[0] * (1.0 + 2.0 * (1.0 - s0[0]))
    infil = limit * fall / (limit + fall)
    c = from_below(lanes, 1, c, ext1)
    from_below(lanes, 0, c, ext0 - infil)
    d = yy[0]
    acc = update(0, 4, d, zero)

    def downward(k, c):
        d = yy[k] + gg[k] * c[0]
        return d, update(k, 4, d, c[1])

    lsend[2] = lax.fori_loop(1, Z, downward, (d, acc), unroll=2)[1]
    h2 = halo(2, 4, 1)

    c = lax.fori_loop(0, Z, functools.partial(assemble, 1), (zero,) * 6, unroll=2)
    finish(c)
    rs[block(1), :] = rs[block(1), :] + (ext0 - infil)
    rs[block(2), :] = rs[block(2), :] + ext1
    for c in h2:
        c.wait_recv()
    lanes = side_terms(2, 4)
    half = Z // 2

    def both_ends(i, c):
        inv_t, b_t, inv_b, b_b = c
        g, inv_t, b_t = eliminate(i, kvs[i], inv_t, b_t, lanes)
        gg[i] = g
        return (inv_t, b_t) + from_below(lanes, Z - 1 - i, (inv_b, b_b))

    inv_t, b_t, inv_b, b_b = lax.fori_loop(0, half, both_ends, (zero,) * 4, unroll=2)
    g = kvs[half] * inv_t
    d_b = (b_b + g * b_t) * inv_b / (1.0 - kvs[half] * g * inv_b)
    d_t = yy[half - 1] + g * d_b
    acc = update(half, 5, d_b, update(half - 1, 5, d_t, zero))

    def outward(i, c):
        d_t, d_b, acc = c
        t, b = half - 1 - i, half + i
        d_t = yy[t] + gg[t + 1] * d_t
        d_b = yy[b] + gg[b] * d_b
        return d_t, d_b, update(b, 5, d_b, update(t, 5, d_t, acc))

    lsend[3] = lax.fori_loop(1, half, outward, (d_t, d_b, acc), unroll=2)[2]
    h3 = halo(3, 5, 1)
    c_pout = pltpu.make_async_copy(pc, p_out, out_sem.at[1])
    c_pout.start()

    def flow(t, u, u_n, m, m_n):
        t_out, t_in = jnp.maximum(t, 0.0), jnp.minimum(t, 0.0)
        return t_out * u + t_in * u_n, t_out * m + t_in * m_n

    def outflows(k, c):
        p1, r1, a1, m1, ga1, gm1, out_a1, out_m1 = c
        p, s, r, w = wet(k, 1)
        a, m = ap[layer(k), :], mp[layer(k), :]
        ga, gm = flow(r1 * r * (p1 - p + 1.0), a1, a, m1, m)
        dg[block(k), :] = out_a1 + (ga - ga1)
        rs[block(k), :] = out_m1 + (gm - gm1)
        hr = 0.5 * r
        f_a, f_m = flow(
            jnp.where(last_lane, 0.0, pltpu.roll(r, LANES - 1, 1) * p - pltpu.roll(w, LANES - 1, 1)),
            a, pltpu.roll(a, LANES - 1, 1), m, pltpu.roll(m, LANES - 1, 1),
        )
        f_a, f_m = hr * f_a, hr * f_m
        u_a, u_m = flow(rp[layer(k, -1), :] * p - wp[layer(k, -1), :], a, ap[layer(k, -1), :], m, mp[layer(k, -1), :])
        d_a, d_m = flow(rp[layer(k, 1), :] * p - wp[layer(k, 1), :], a, ap[layer(k, 1), :], m, mp[layer(k, 1), :])
        out_a = hr * (u_a + d_a) + (f_a - pltpu.roll(f_a, 1, 1))
        out_m = hr * (u_m + d_m) + (f_m - pltpu.roll(f_m, 1, 1))
        return p, r, a, m, ga, gm, out_a, out_m

    c = lax.fori_loop(0, Z, outflows, (zero,) * 8)
    dg[block(Z), :] = c[6] - c[4]
    rs[block(Z), :] = c[7] - c[5]
    for k, ext in ((0, ext0), (1, ext1)):
        dg[block(k + 1), :] = dg[block(k + 1), :] + ext * ap[layer(k), :]
        rs[block(k + 1), :] = rs[block(k + 1), :] + ext * mp[layer(k), :]

    for c in h1 + h3:
        c.wait_recv()
    lane_am = lane_halo(1)
    moment_edges = (
        (lane_am, lsend[1], pltpu.roll(lane_am, HALF, 1), pltpu.roll(lsend[1], HALF, 1)),
        (drecv[2], usend[2], drecv[3], usend[3]),
        (urecv[2], dsend[2], urecv[3], dsend[3]),
    )
    terms = []
    for (hr, hw, own_r, own_p), (ha, own_a, hm, own_m) in zip(edge_state(3, 5), moment_edges):
        f_a, f_m = flow(hr * own_p - hw, own_a, ha, own_m, hm)
        terms.append((0.5 * own_r * f_a, 0.5 * own_r * f_m))
    add_rows(dg, terms[1][0], terms[2][0])
    add_rows(rs, terms[1][1], terms[2][1])

    def ages(k, _):
        a, m = age[k], mp[layer(k), :]
        out_a = dg[block(k + 1), :] + spread(k, terms[0][0])
        out_m = rs[block(k + 1), :] + spread(k, terms[0][1])
        old = 0.05 + 0.4 * s0[k]
        inv = 1.0 / (0.05 + 0.4 * sc[k])
        a2 = (old * a - 0.2 * out_a) * inv + 0.2
        av[k] = a2
        vv[k] = (old * m - 0.2 * out_m) * inv + (0.4 - a2) * a2
        return 0

    outs = []
    chunk = Z // 4
    for n in range(4):
        lax.fori_loop(n * chunk, (n + 1) * chunk, ages, 0, unroll=2)
        for i, (src, dst) in enumerate(((av, a_out), (vv, v_out))):
            at = pl.ds(n * chunk, chunk)
            c = pltpu.make_async_copy(src.at[at], dst.at[at], out_sem.at[2 + 2 * n + i])
            c.start()
            outs.append(c)
    for c in sends:
        c.wait_send()
    for c in outs + [c_land, c_pout]:
        c.wait()


def shards(GX, GY, pressure, ksat, age_mean, age_var, remap, forcing, land_state, veg_class, veg_table):
    Z, X, _ = pressure.shape
    f32 = functools.partial(jax.ShapeDtypeStruct, dtype=F32)
    padded = pltpu.VMEM((Z * (X + 2 * PAD), LANES), F32)
    flat = pltpu.VMEM(((Z + 1) * X, LANES), F32)
    plain = pltpu.VMEM((Z + 1, X, LANES), F32)
    exact = pltpu.VMEM((Z, X, LANES), F32)
    dma = pltpu.SemaphoreType.DMA
    any_spec = pl.BlockSpec(memory_space=pl.ANY)
    return pl.pallas_call(
        functools.partial(kernel, Z, X, GX, GY),
        out_shape=(
            f32((Z, X, LANES)), f32((Z, X, LANES)), f32((Z, X, LANES)), f32(land_state.shape),
        ),
        in_specs=[any_spec] * 9,
        out_specs=(any_spec,) * 4,
        scratch_shapes=[padded] * 4 + [flat] * 2 + [exact] * 4 + [plain] * 3 + [exact] * 4 + [
            pltpu.VMEM((1, X), jnp.int32),
            pltpu.VMEM(forcing.shape, F32),
            pltpu.VMEM(land_state.shape, F32),
            pltpu.VMEM(veg_class.shape, jnp.int32),
            pltpu.SMEM(veg_table.shape, F32),
            pltpu.VMEM(land_state.shape, F32),
            pltpu.VMEM((GY, 8, LANES), F32),
            pltpu.VMEM((GY, 8, LANES), F32),
            pltpu.VMEM((GY, 16, LANES), F32),
            pltpu.VMEM((GY, 16, LANES), F32),
            pltpu.VMEM((4, X, LANES), F32),
            pltpu.VMEM((4, 2, X, LANES), F32),
            pltpu.VMEM((6, Z, LANES), F32),
            pltpu.VMEM((6, Z, LANES), F32),
            pltpu.VMEM((6, Z, LANES), F32),
            pltpu.VMEM((6, Z, LANES), F32),
            dma((9,)), dma((10,)), dma((GY,)), dma((GY,)), dma((GY,)), dma((GY,)), dma((4, 4)), dma((4, 4)),
        ],
        compiler_params=pltpu.CompilerParams(
            collective_id=0, has_side_effects=True, vmem_limit_bytes=62 * 1024 * 1024
        ),
    )(pressure, ksat, age_mean, age_var, remap.reshape(1, X), forcing, land_state, veg_class, veg_table)


def solution(mesh):
    field = P(None, "gx", "gy")
    return jax.shard_map(
        functools.partial(shards, mesh.shape["gx"], mesh.shape["gy"]),
        mesh=mesh,
        in_specs=(field, field, field, field, P("gx", "gy"), field, field, P("gx", "gy"), P()),
        out_specs=(field, field, field, field),
        check_vma=False,
    )
```

```python
import functools
import math

import jax
import jax.numpy as jnp
from jax import lax
from jax.experimental import pallas as pl
from jax.experimental.pallas import tpu as pltpu
from jax.sharding import PartitionSpec as P

LANES = 128
HALF = 64
PAD = 8
SLOTS = 4
F32 = jnp.float32
BF16 = jnp.bfloat16
MESH = pl.DeviceIdType.MESH


def sigmoid(x):
    return 0.5 * jnp.tanh(0.5 * x) + 0.5


def root_conduct(s, ksat):
    x = ksat * (0.05 + s * s)
    return x * lax.rsqrt(x)


def iota(shape, dim):
    return lax.broadcasted_iota(jnp.int32, shape, dim)


def pieces(x):
    high = x.astype(BF16)
    rest = x - high.astype(F32)
    mid = rest.astype(BF16)
    return high, mid, (rest - mid.astype(F32)).astype(BF16)


def pick_rows(one_hot, x):
    n = x.shape[1]
    out = jnp.dot(one_hot.astype(BF16), jnp.concatenate(pieces(x), axis=1), preferred_element_type=F32)
    return (out[:, 2 * n:] + out[:, n:2 * n]) + out[:, :n]


def kernel(
    Z, X, GX, GY,
    p_hbm, k_hbm, a_hbm, v_hbm, remap_hbm, forc_hbm, state_hbm, veg_hbm, table_hbm,
    pc, landn, dg, rs, s0, sc, age, mom, terms_out,
    rp, wp, ap, mp, ks, gg, yy, kvs, var,
    remap, forc, state, veg, table,
    osend, orecv, fsend, frecv,
    lsend, lrecv, usend, urecv, dsend, drecv,
    load_sem, o_ssem, o_rsem, f_ssem, f_rsem, h_ssem, h_rsem,
):
    gx, gy = lax.axis_index("gx"), lax.axis_index("gy")
    up, down = lax.rem(gx + GX - 1, GX), lax.rem(gx + 1, GX)
    left, right = lax.rem(gy + GY - 1, GY), lax.rem(gy + 1, GY)
    stride = X + 2 * PAD
    side = math.isqrt(GY)

    def layer(k, shift=0):
        return pl.ds(pl.multiple_of(k * stride, 8) + (PAD + shift), X)

    def block(k):
        return pl.ds(pl.multiple_of(k * X, 8), X)

    def far(o):
        dy, dx = o // side, o % side
        return min(dy, side - dy) + min(dx, side - dx)

    offsets = sorted(range(1, GY), key=lambda o: -far(o))
    my_y, my_x = gy // side, lax.rem(gy, side)
    peers = {
        o: lax.rem(my_y + o // side, side) * side + lax.rem(my_x + o % side, side) for o in offsets
    }

    def load(src, dst, n):
        c = pltpu.make_async_copy(src, dst, load_sem.at[n])
        c.start()
        return c

    barrier = pltpu.get_barrier_semaphore()
    for o in offsets:
        pl.semaphore_signal(barrier, inc=1, device_id={"gy": peers[o]}, device_id_type=MESH)
    for d in (up, down):
        pl.semaphore_signal(barrier, inc=1, device_id={"gx": d}, device_id_type=MESH)
    c_remap = load(remap_hbm, remap, 0)
    c_forc = load(forc_hbm, forc, 3)
    c_state = load(state_hbm, state, 4)
    c_veg = load(veg_hbm, veg, 5)
    c_table = load(table_hbm, table, 6)
    c_p = load(p_hbm, pc, 1)
    c_k = load(k_hbm, ks, 2)
    c_a = load(a_hbm, age, 7)
    c_v = load(v_hbm, var, 8)

    def send(src, dst, ssem, rsem, where):
        c = pltpu.make_async_remote_copy(
            src_ref=src, dst_ref=dst, send_sem=ssem, recv_sem=rsem,
            device_id=where, device_id_type=MESH,
        )
        c.start()
        return c

    lane = iota((X, LANES), 1)
    pair = lane >> 1
    first_lane, last_lane = lane == 0, lane == LANES - 1
    edge = first_lane | last_lane
    even = (lane & 1) == 0
    zero = jnp.zeros((X, LANES), F32)
    pad = jnp.zeros((PAD, LANES), F32)

    c_remap.wait()
    bits = X.bit_length() - 1
    code_row = remap[...]
    eye = iota((X, X), 0) == iota((X, X), 1)
    code_col = jnp.sum(jnp.where(eye, jnp.broadcast_to(code_row, (X, X)), 0), axis=1, keepdims=True)
    dest_row, dest_col = code_row >> bits, code_col >> bits
    slot_col = code_col & (X - 1)
    same = jnp.broadcast_to(dest_col, (X, X)) == jnp.broadcast_to(dest_row, (X, X))
    rank_row = jnp.sum(jnp.where(same & (iota((X, X), 0) < iota((X, X), 1)), 1, 0), axis=0, keepdims=True)
    rank_col = jnp.sum(jnp.where(same & (iota((X, X), 1) < iota((X, X), 0)), 1, 0), axis=1, keepdims=True)
    rows = 8 * GY
    row_id = iota((rows, X), 0)
    row_key = (row_id >> 3) * SLOTS + (row_id & (SLOTS - 1))
    tile_of_row = (row_key == jnp.broadcast_to(dest_row * SLOTS + rank_row, (rows, X))).astype(BF16)
    slot_of_tile = (jnp.broadcast_to(slot_col, (X, LANES)) == iota((X, LANES), 1)).astype(BF16)
    osend[...] = jnp.dot(tile_of_row, slot_of_tile, preferred_element_type=F32).reshape(GY, 8, LANES)

    pl.semaphore_wait(barrier, GY + 1)

    sends = []
    o_copies = [
        send(osend.at[peers[o]], orecv.at[gy], o_ssem.at[o], o_rsem.at[o], {"gy": peers[o]}) for o in offsets
    ]
    sends += o_copies
    orecv[gy] = osend[gy]

    row_of_tile = jnp.broadcast_to(dest_col * 8 + rank_col, (X, rows))
    take = jnp.concatenate(
        [(row_of_tile + n == iota((X, rows), 1)).astype(F32) for n in (0, SLOTS)], axis=0
    )

    c_veg.wait()
    c_table.wait()
    c_forc.wait()
    c_state.wait()
    cls = veg[...]
    nveg = table.shape[1]
    par = [jnp.full((X, LANES), table[i, 0], F32) for i in range(5)]
    for v in range(1, nveg):
        hit = cls == v
        par = [jnp.where(hit, table[i, v], par[i]) for i in range(5)]
    albedo, conduct, capacity, et_factor, decay = par
    skin = (state[0] + 0.5 * ((1.0 - albedo) * 2.0 * forc[0] + 0.5 * forc[1] + forc[2])) / 1.5
    soft = jnp.maximum(skin, 0.0) + jnp.log(1.0 + jnp.exp(-jnp.abs(skin)))
    demand = conduct * soft * (1.0 + forc[4]) * (1.0 - 0.5 * forc[3]) / (0.5 + forc[5])
    wetted = state[1] + forc[6]
    drip = jnp.maximum(wetted - capacity, 0.0)
    canopy = (wetted - drip) * capacity / (demand + capacity)
    through = drip + 0.5 * forc[6]
    draw0 = 0.5 * et_factor * demand / (1.0 + decay)
    draw1 = draw0 * decay
    landn[0] = skin
    landn[1] = canopy
    fields = jnp.concatenate([draw0, draw1, through], axis=1)

    for ref in (rp, wp, ap, mp):
        for k in range(Z):
            ref[k * stride:k * stride + PAD, :] = pad
            ref[k * stride + PAD + X:(k + 1) * stride, :] = pad

    def edge_rows(k, n, value):
        usend[n, pl.ds(k, 1), :] = value[0:1]
        dsend[n, pl.ds(k, 1), :] = value[X - 1:X]

    def wet(k, turn):
        p = pc[k]
        s = sigmoid(p)
        r = root_conduct(s, ks[k])
        w = r * p
        (sc if turn else s0)[k] = s
        rp[layer(k), :] = r
        wp[layer(k), :] = w
        return p, s, r, w

    def near(ref, k, value):
        return (
            (ref[layer(k, -1), :] + ref[layer(k, 1), :])
            + jnp.where(first_lane, 0.0, pltpu.roll(value, 1, 1))
            + jnp.where(last_lane, 0.0, pltpu.roll(value, LANES - 1, 1))
        )

    def assemble(turn, k, c):
        p1, r1, kv1, qv1, diag1, res1 = c[:6]
        p, s, r, w = wet(k, turn)
        kv = r1 * r
        qv = kv * (p1 - p + 1.0)
        dg[block(k), :] = diag1 + kv1 + kv
        rs[block(k), :] = res1 + (qv - qv1)
        kvs[k] = kv
        sum1, sum2 = near(rp, k, r), near(wp, k, w)
        hr = 0.5 * r
        diag = 2.0 * s * (1.0 - s) + hr * sum1
        res = hr * (p * sum1 - sum2)
        if turn:
            res = res + 2.0 * (s - s0[k])
            return p, r, kv, qv, diag, res
        edge_rows(k, 0, p)
        edge_rows(k, 1, ks[k])
        acc = jnp.where(pair == k, pltpu.roll(p, 2 * k + 1, 1), c[6])
        acc = jnp.where(pair == k + HALF // 2, pltpu.roll(ks[k], HALF + 2 * k + 1, 1), acc)
        return p, r, kv, qv, diag, res, acc

    def finish(c):
        _, _, kv1, qv1, diag1, res1 = c[:6]
        dg[block(Z), :] = diag1 + kv1
        rs[block(Z), :] = res1 - qv1
        kvs[Z] = zero

    c_p.wait()
    c_k.wait()
    c = lax.fori_loop(0, Z, functools.partial(assemble, 0), (zero,) * 7, unroll=4)
    lsend[0] = c[6]
    finish(c)

    def halo(phase, row0, nrows):
        cs = [
            send(lsend.at[phase], lrecv.at[phase, 0], h_ssem.at[phase, 0], h_rsem.at[phase, 0], {"gy": right}),
            send(lsend.at[phase], lrecv.at[phase, 1], h_ssem.at[phase, 1], h_rsem.at[phase, 1], {"gy": left}),
            send(usend.at[pl.ds(row0, nrows)], urecv.at[pl.ds(row0, nrows)],
                 h_ssem.at[phase, 2], h_rsem.at[phase, 2], {"gx": up}),
            send(dsend.at[pl.ds(row0, nrows)], drecv.at[pl.ds(row0, nrows)],
                 h_ssem.at[phase, 3], h_rsem.at[phase, 3], {"gx": down}),
        ]
        sends.extend(cs)
        return cs

    h0 = halo(0, 0, 2)

    for c in o_copies:
        c.wait_recv()
    packed = pick_rows(orecv[...].reshape(rows, LANES)[:, :X], fields)
    low = (iota((rows, LANES), 0) & 7) < SLOTS
    first_half = jnp.where(low, packed[:, :LANES], packed[:, LANES:2 * LANES])
    fsend[:, 0:8, :] = first_half.reshape(GY, 8, LANES)
    fsend[:, 8:16, :] = packed[:, 2 * LANES:].reshape(GY, 8, LANES)
    f_copies = [
        send(fsend.at[peers[o]], frecv.at[gy], f_ssem.at[o], f_rsem.at[o], {"gy": peers[o]}) for o in offsets
    ]
    sends += f_copies
    frecv[gy] = fsend[gy]

    c_a.wait()
    c_v.wait()

    def moments(k, acc):
        a = age[k]
        m = var[k] + a * a
        ap[layer(k), :] = a
        mp[layer(k), :] = m
        mom[k] = m
        edge_rows(k, 2, a)
        edge_rows(k, 3, m)
        acc = jnp.where(pair == k, pltpu.roll(a, 2 * k + 1, 1), acc)
        return jnp.where(pair == k + HALF // 2, pltpu.roll(m, HALF + 2 * k + 1, 1), acc)

    lsend[1] = lax.fori_loop(0, Z, moments, zero, unroll=4)
    h1 = halo(1, 2, 2)

    def lane_halo(phase):
        return jnp.where(
            even, pltpu.roll(lrecv[phase, 1], LANES - 1, 1), pltpu.roll(lrecv[phase, 0], 1, 1)
        )

    for c in h0:
        c.wait_recv()
    lane_pk = lane_halo(0)
    inside = jnp.where(even, jnp.where(gy < GY - 1, 1.0, 0.0), jnp.where(gy > 0, 1.0, 0.0))
    above_in = jnp.where(gx > 0, 1.0, 0.0)
    below_in = jnp.where(gx < GX - 1, 1.0, 0.0)

    def compact_k(packed):
        return jnp.where(lane < HALF, pltpu.roll(packed, HALF, 1), 1.0)

    edge_k = (
        (compact_k(lane_pk), compact_k(lsend[0]), inside),
        (drecv[1], usend[1], above_in),
        (urecv[1], dsend[1], below_in),
    )

    def edge_p(phase, n):
        return ((lane_halo(phase), lsend[phase]), (drecv[n], usend[n]), (urecv[n], dsend[n]))

    def edge_state(phase, n):
        out = []
        for (hk, ok, inner), (hp, op) in zip(edge_k, edge_p(phase, n)):
            hr = root_conduct(sigmoid(hp), hk) * inner
            out.append((hr, hr * hp, root_conduct(sigmoid(op), ok), op))
        return out

    def add_rows(ref, above, below):
        for row, value in ((0, above), (X - 1, below)):
            at = pl.ds(X + row, Z, stride=X)
            ref[at, :] = ref[at, :] + value

    def spread(k, compact):
        return jnp.where(edge, pltpu.roll(compact, LANES - 1 - 2 * k, 1), 0.0)

    def side_terms(phase, n):
        terms = [
            (0.5 * own_r * hr, 0.5 * own_r * (own_p * hr - hw)) for hr, hw, own_r, own_p in edge_state(phase, n)
        ]
        add_rows(dg, terms[1][0], terms[2][0])
        add_rows(rs, terms[1][1], terms[2][1])
        return terms[0]

    def eliminate(k, coupling, inv, b, lanes, source=None):
        diag = dg[block(k + 1), :] + spread(k, lanes[0])
        res = rs[block(k + 1), :] + spread(k, lanes[1])
        if source is not None:
            res = res + source
        g = coupling * inv
        b = g * b - res
        inv = 1.0 / (diag - coupling * g)
        yy[k] = b * inv
        return g, inv, b

    def from_below(lanes, k, c, source=None):
        g, inv, b = eliminate(k, kvs[k + 1], *c, lanes, source)
        gg[k + 1] = g
        return inv, b

    def update(k, n, d, acc):
        p = pc[k] + d
        pc[k] = p
        edge_rows(k, n, p)
        return jnp.where(pair == k, pltpu.roll(p, 2 * k + 1, 1), acc)

    lanes = side_terms(0, 0)
    c = lax.fori_loop(0, Z - 2, lambda i, c: from_below(lanes, Z - 1 - i, c), (zero, zero), unroll=4)
    for f in f_copies:
        f.wait_recv()
    got = pick_rows(
        take,
        jnp.concatenate(
            [frecv[:, 0:8, :].reshape(rows, LANES), frecv[:, 8:16, :].reshape(rows, LANES)], axis=1
        ),
    )
    ext0 = got[:X, :LANES] * s0[0]
    ext1 = got[X:, :LANES] * s0[1]
    fall = got[:X, LANES:]
    limit = ks[0] * (1.0 + 2.0 * (1.0 - s0[0]))
    infil = limit * fall / (limit + fall)
    c = from_below(lanes, 1, c, ext1)
    from_below(lanes, 0, c, ext0 - infil)
    d = yy[0]
    acc = update(0, 4, d, zero)

    def downward(k, c):
        d = yy[k] + gg[k] * c[0]
        return d, update(k, 4, d, c[1])

    lsend[2] = lax.fori_loop(1, Z, downward, (d, acc), unroll=31)[1]
    h2 = halo(2, 4, 1)

    c = lax.fori_loop(0, Z, functools.partial(assemble, 1), (zero,) * 6, unroll=4)
    finish(c)
    rs[block(1), :] = rs[block(1), :] + (ext0 - infil)
    rs[block(2), :] = rs[block(2), :] + ext1
    for c in h2:
        c.wait_recv()
    lanes = side_terms(2, 4)
    half = Z // 2

    def both_ends(i, c):
        inv_t, b_t, inv_b, b_b = c
        g, inv_t, b_t = eliminate(i, kvs[i], inv_t, b_t, lanes)
        gg[i] = g
        return (inv_t, b_t) + from_below(lanes, Z - 1 - i, (inv_b, b_b))

    inv_t, b_t, inv_b, b_b = lax.fori_loop(0, half, both_ends, (zero,) * 4, unroll=16)
    g = kvs[half] * inv_t
    d_b = (b_b + g * b_t) * inv_b / (1.0 - kvs[half] * g * inv_b)
    d_t = yy[half - 1] + g * d_b
    acc = update(half, 5, d_b, update(half - 1, 5, d_t, zero))

    def outward(i, c):
        d_t, d_b, acc = c
        t, b = half - 1 - i, half + i
        d_t = yy[t] + gg[t + 1] * d_t
        d_b = yy[b] + gg[b] * d_b
        return d_t, d_b, update(b, 5, d_b, update(t, 5, d_t, acc))

    lsend[3] = lax.fori_loop(1, half, outward, (d_t, d_b, acc), unroll=15)[2]
    h3 = halo(3, 5, 1)

    def flow(t, u, u_n, m, m_n):
        t_out, t_in = jnp.maximum(t, 0.0), jnp.minimum(t, 0.0)
        return t_out * u + t_in * u_n, t_out * m + t_in * m_n

    def outflows(k, c):
        p1, r1, a1, m1, ga1, gm1, out_a1, out_m1 = c
        p, s, r, w = wet(k, 1)
        a, m = ap[layer(k), :], mp[layer(k), :]
        ga, gm = flow(r1 * r * (p1 - p + 1.0), a1, a, m1, m)
        dg[block(k), :] = out_a1 + (ga - ga1)
        rs[block(k), :] = out_m1 + (gm - gm1)
        hr = 0.5 * r
        f_a, f_m = flow(
            jnp.where(last_lane, 0.0, pltpu.roll(r, LANES - 1, 1) * p - pltpu.roll(w, LANES - 1, 1)),
            a, pltpu.roll(a, LANES - 1, 1), m, pltpu.roll(m, LANES - 1, 1),
        )
        f_a, f_m = hr * f_a, hr * f_m
        u_a, u_m = flow(rp[layer(k, -1), :] * p - wp[layer(k, -1), :], a, ap[layer(k, -1), :], m, mp[layer(k, -1), :])
        d_a, d_m = flow(rp[layer(k, 1), :] * p - wp[layer(k, 1), :], a, ap[layer(k, 1), :], m, mp[layer(k, 1), :])
        out_a = hr * (u_a + d_a) + (f_a - pltpu.roll(f_a, 1, 1))
        out_m = hr * (u_m + d_m) + (f_m - pltpu.roll(f_m, 1, 1))
        return p, r, a, m, ga, gm, out_a, out_m

    c = lax.fori_loop(0, Z, outflows, (zero,) * 8, unroll=2)
    dg[block(Z), :] = c[6] - c[4]
    rs[block(Z), :] = c[7] - c[5]
    for k, ext in ((0, ext0), (1, ext1)):
        dg[block(k + 1), :] = dg[block(k + 1), :] + ext * ap[layer(k), :]
        rs[block(k + 1), :] = rs[block(k + 1), :] + ext * mp[layer(k), :]

    for c in h1 + h3:
        c.wait_recv()
    lane_am = lane_halo(1)
    moment_edges = (
        (lane_am, lsend[1], pltpu.roll(lane_am, HALF, 1), pltpu.roll(lsend[1], HALF, 1)),
        (drecv[2], usend[2], drecv[3], usend[3]),
        (urecv[2], dsend[2], urecv[3], dsend[3]),
    )
    terms = []
    for (hr, hw, own_r, own_p), (ha, own_a, hm, own_m) in zip(edge_state(3, 5), moment_edges):
        f_a, f_m = flow(hr * own_p - hw, own_a, ha, own_m, hm)
        terms.append((0.5 * own_r * f_a, 0.5 * own_r * f_m))
    add_rows(dg, terms[1][0], terms[2][0])
    add_rows(rs, terms[1][1], terms[2][1])

    terms_out[0] = terms[0][0]
    terms_out[1] = terms[0][1]
    for c in sends:
        c.wait_send()


def finale(
    Z, X, pc, landn, dg, rs, s0, sc, age, mom, terms, p_out, a_out, v_out, land_out, av, vv, out_sem
):
    copies = []

    def store(src, dst):
        c = pltpu.make_async_copy(src, dst, out_sem.at[len(copies)])
        c.start()
        copies.append(c)

    store(pc, p_out)
    store(landn, land_out)
    lane = iota((X, LANES), 1)
    edge = (lane == 0) | (lane == LANES - 1)

    def block(k):
        return pl.ds(pl.multiple_of(k * X, 8), X)

    def spread(k, compact):
        return jnp.where(edge, pltpu.roll(compact, LANES - 1 - 2 * k, 1), 0.0)

    def ages(k, _):
        a, m = age[k], mom[k]
        out_a = dg[block(k + 1), :] + spread(k, terms[0])
        out_m = rs[block(k + 1), :] + spread(k, terms[1])
        old = 0.05 + 0.4 * s0[k]
        inv = 1.0 / (0.05 + 0.4 * sc[k])
        a2 = (old * a - 0.2 * out_a) * inv + 0.2
        av[k] = a2
        vv[k] = (old * m - 0.2 * out_m) * inv + (0.4 - a2) * a2
        return 0

    chunk = Z // 4
    for n in range(4):
        lax.fori_loop(n * chunk, (n + 1) * chunk, ages, 0, unroll=8)
        at = pl.ds(n * chunk, chunk)
        store(av.at[at], a_out.at[at])
        store(vv.at[at], v_out.at[at])
    for c in copies:
        c.wait()


def shards(GX, GY, pressure, ksat, age_mean, age_var, remap, forcing, land_state, veg_class, veg_table):
    Z, X, _ = pressure.shape
    f32 = functools.partial(jax.ShapeDtypeStruct, dtype=F32)
    padded = pltpu.VMEM((Z * (X + 2 * PAD), LANES), F32)
    flat = pltpu.VMEM(((Z + 1) * X, LANES), F32)
    plain = pltpu.VMEM((Z + 1, X, LANES), F32)
    land = pltpu.VMEM(land_state.shape, F32)
    exact = pltpu.VMEM((Z, X, LANES), F32)
    dma = pltpu.SemaphoreType.DMA
    any_spec = pl.BlockSpec(memory_space=pl.ANY)
    vmem_spec = pl.BlockSpec(memory_space=pltpu.VMEM)
    inputs = (pressure, ksat, age_mean, age_var, remap.reshape(1, X), forcing, land_state, veg_class, veg_table)
    held = pl.pallas_call(
        functools.partial(kernel, Z, X, GX, GY),
        out_shape=(exact, land, flat, flat, exact, exact, exact, exact, pltpu.VMEM((2, X, LANES), F32)),
        in_specs=[any_spec] * 9,
        out_specs=(vmem_spec,) * 9,
        scratch_shapes=[padded] * 4 + [exact] + [plain] * 3 + [exact] + [
            pltpu.VMEM((1, X), jnp.int32),
            pltpu.VMEM(forcing.shape, F32),
            pltpu.VMEM(land_state.shape, F32),
            pltpu.VMEM(veg_class.shape, jnp.int32),
            pltpu.SMEM(veg_table.shape, F32),
            pltpu.VMEM((GY, 8, LANES), F32),
            pltpu.VMEM((GY, 8, LANES), F32),
            pltpu.VMEM((GY, 16, LANES), F32),
            pltpu.VMEM((GY, 16, LANES), F32),
            pltpu.VMEM((4, X, LANES), F32),
            pltpu.VMEM((4, 2, X, LANES), F32),
            pltpu.VMEM((6, Z, LANES), F32),
            pltpu.VMEM((6, Z, LANES), F32),
            pltpu.VMEM((6, Z, LANES), F32),
            pltpu.VMEM((6, Z, LANES), F32),
            dma((9,)), dma((GY,)), dma((GY,)), dma((GY,)), dma((GY,)), dma((4, 4)), dma((4, 4)),
        ],
        compiler_params=pltpu.CompilerParams(
            collective_id=0, has_side_effects=True, vmem_limit_bytes=24 * 1024 * 1024
        ),
    )(*(pltpu.with_memory_space_constraint(x, pltpu.HBM) for x in inputs))
    return pl.pallas_call(
        functools.partial(finale, Z, X),
        out_shape=(
            f32((Z, X, LANES)), f32((Z, X, LANES)), f32((Z, X, LANES)), f32(land_state.shape),
        ),
        in_specs=[vmem_spec] * 9,
        out_specs=(any_spec,) * 4,
        scratch_shapes=[exact, exact, dma((10,))],
        compiler_params=pltpu.CompilerParams(vmem_limit_bytes=8 * 1024 * 1024),
    )(*held)


def solution(mesh):
    field = P(None, "gx", "gy")
    return jax.shard_map(
        functools.partial(shards, mesh.shape["gx"], mesh.shape["gy"]),
        mesh=mesh,
        in_specs=(field, field, field, field, P("gx", "gy"), field, field, P("gx", "gy"), P()),
        out_specs=(field, field, field, field),
        check_vma=False,
    )
```

```python
import functools
import math

import jax
import jax.numpy as jnp
from jax import lax
from jax.experimental import pallas as pl
from jax.experimental.pallas import tpu as pltpu
from jax.sharding import PartitionSpec as P

LANES = 128
HALF = 64
PAD = 8
SLOTS = 4
F32 = jnp.float32
BF16 = jnp.bfloat16
MESH = pl.DeviceIdType.MESH


def sigmoid(x):
    return 0.5 * jnp.tanh(0.5 * x) + 0.5


def root_conduct(s, ksat):
    x = ksat * (0.05 + s * s)
    return x * lax.rsqrt(x)


def iota(shape, dim):
    return lax.broadcasted_iota(jnp.int32, shape, dim)


def pieces(x):
    high = x.astype(BF16)
    rest = x - high.astype(F32)
    mid = rest.astype(BF16)
    return high, mid, (rest - mid.astype(F32)).astype(BF16)


def pick_rows(one_hot, x):
    n = x.shape[1]
    out = jnp.dot(one_hot.astype(BF16), jnp.concatenate(pieces(x), axis=1), preferred_element_type=F32)
    return (out[:, 2 * n:] + out[:, n:2 * n]) + out[:, :n]


def kernel(
    Z, X, GX, GY,
    p_hbm, k_hbm, a_hbm, v_hbm, remap_hbm, forc_hbm, state_hbm, veg_hbm, table_hbm,
    pc, landn, dg, rs, s0, sc, age, mom, terms_out,
    rp, wp, ap, mp, ks, gg, yy, kvs, var, slope, inv1,
    remap, forc, state, veg, table,
    osend, orecv, fsend, frecv, tiles,
    lsend, lrecv, usend, urecv, dsend, drecv,
    load_sem, o_ssem, o_rsem, f_ssem, f_rsem, h_ssem, h_rsem,
):
    gx, gy = lax.axis_index("gx"), lax.axis_index("gy")
    up, down = lax.rem(gx + GX - 1, GX), lax.rem(gx + 1, GX)
    left, right = lax.rem(gy + GY - 1, GY), lax.rem(gy + 1, GY)
    stride = X + 2 * PAD
    side = math.isqrt(GY)

    def layer(k, shift=0):
        return pl.ds(pl.multiple_of(k * stride, 8) + (PAD + shift), X)

    def block(k):
        return pl.ds(pl.multiple_of(k * X, 8), X)

    def far(o):
        dy, dx = o // side, o % side
        return min(dy, side - dy) + min(dx, side - dx)

    offsets = sorted(range(1, GY), key=lambda o: -far(o))
    my_y, my_x = gy // side, lax.rem(gy, side)
    peers = {
        o: lax.rem(my_y + o // side, side) * side + lax.rem(my_x + o % side, side) for o in offsets
    }

    def load(src, dst, n):
        c = pltpu.make_async_copy(src, dst, load_sem.at[n])
        c.start()
        return c

    barrier = pltpu.get_barrier_semaphore()
    for o in offsets:
        pl.semaphore_signal(barrier, inc=1, device_id={"gy": peers[o]}, device_id_type=MESH)
    for d in (up, down):
        pl.semaphore_signal(barrier, inc=1, device_id={"gx": d}, device_id_type=MESH)
    c_remap = load(remap_hbm, remap, 0)
    c_forc = load(forc_hbm, forc, 3)
    c_state = load(state_hbm, state, 4)
    c_veg = load(veg_hbm, veg, 5)
    c_table = load(table_hbm, table, 6)
    c_p = load(p_hbm, pc, 1)
    c_k = load(k_hbm, ks, 2)
    c_a = load(a_hbm, age, 7)
    c_v = load(v_hbm, var, 8)

    def send(src, dst, ssem, rsem, where):
        c = pltpu.make_async_remote_copy(
            src_ref=src, dst_ref=dst, send_sem=ssem, recv_sem=rsem,
            device_id=where, device_id_type=MESH,
        )
        c.start()
        return c

    lane = iota((X, LANES), 1)
    pair = lane >> 1
    first_lane, last_lane = lane == 0, lane == LANES - 1
    edge = first_lane | last_lane
    even = (lane & 1) == 0
    zero = jnp.zeros((X, LANES), F32)
    pad = jnp.zeros((PAD, LANES), F32)

    c_remap.wait()
    bits = X.bit_length() - 1
    code_row = remap[...]
    eye = iota((X, X), 0) == iota((X, X), 1)
    code_col = jnp.sum(jnp.where(eye, jnp.broadcast_to(code_row, (X, X)), 0), axis=1, keepdims=True)
    dest_row, dest_col = code_row >> bits, code_col >> bits
    slot_col = code_col & (X - 1)
    same = jnp.broadcast_to(dest_col, (X, X)) == jnp.broadcast_to(dest_row, (X, X))
    rank_row = jnp.sum(jnp.where(same & (iota((X, X), 0) < iota((X, X), 1)), 1, 0), axis=0, keepdims=True)
    rank_col = jnp.sum(jnp.where(same & (iota((X, X), 1) < iota((X, X), 0)), 1, 0), axis=1, keepdims=True)
    rows = 8 * GY
    row_id = iota((rows, X), 0)
    row_key = (row_id >> 3) * SLOTS + (row_id & (SLOTS - 1))
    tile_of_row = (row_key == jnp.broadcast_to(dest_row * SLOTS + rank_row, (rows, X))).astype(BF16)
    slot_of_tile = (jnp.broadcast_to(slot_col, (X, LANES)) == iota((X, LANES), 1)).astype(BF16)
    osend[...] = jnp.dot(tile_of_row, slot_of_tile, preferred_element_type=F32).reshape(GY, 8, LANES)

    pl.semaphore_wait(barrier, GY + 1)

    sends = []
    o_copies = [
        send(osend.at[peers[o]], orecv.at[gy], o_ssem.at[o], o_rsem.at[o], {"gy": peers[o]}) for o in offsets
    ]
    sends += o_copies
    orecv[gy] = osend[gy]

    row_of_tile = jnp.broadcast_to(dest_col * 8 + rank_col, (X, rows))
    take = (row_of_tile == iota((X, rows), 1)).astype(F32)
    tiles[...] = jnp.zeros_like(tiles)

    c_veg.wait()
    c_table.wait()
    c_forc.wait()
    c_state.wait()
    cls = veg[...]
    nveg = table.shape[1]
    par = [jnp.full((X, LANES), table[i, 0], F32) for i in range(5)]
    for v in range(1, nveg):
        hit = cls == v
        par = [jnp.where(hit, table[i, v], par[i]) for i in range(5)]
    albedo, conduct, capacity, et_factor, decay = par
    skin = (state[0] + 0.5 * ((1.0 - albedo) * 2.0 * forc[0] + 0.5 * forc[1] + forc[2])) / 1.5
    soft = jnp.maximum(skin, 0.0) + jnp.log(1.0 + jnp.exp(-jnp.abs(skin)))
    demand = conduct * soft * (1.0 + forc[4]) * (1.0 - 0.5 * forc[3]) / (0.5 + forc[5])
    wetted = state[1] + forc[6]
    drip = jnp.maximum(wetted - capacity, 0.0)
    canopy = (wetted - drip) * capacity / (demand + capacity)
    through = drip + 0.5 * forc[6]
    draw0 = 0.5 * et_factor * demand / (1.0 + decay)
    draw1 = draw0 * decay
    landn[0] = skin
    landn[1] = canopy
    fields = jnp.concatenate([draw0, draw1, through], axis=1)

    for ref in (rp, wp, ap, mp):
        for k in range(Z):
            ref[k * stride:k * stride + PAD, :] = pad
            ref[k * stride + PAD + X:(k + 1) * stride, :] = pad

    def edge_rows(k, n, value):
        usend[n, pl.ds(k, 1), :] = value[0:1]
        dsend[n, pl.ds(k, 1), :] = value[X - 1:X]

    def wet(k, turn, change=None):
        p = pc[k]
        if change is not None:
            p = p + slope[k] * change
            pc[k] = p
        s = sigmoid(p)
        r = root_conduct(s, ks[k])
        w = r * p
        (sc if turn else s0)[k] = s
        rp[layer(k), :] = r
        wp[layer(k), :] = w
        return p, s, r, w

    def near(ref, k, value):
        return (
            (ref[layer(k, -1), :] + ref[layer(k, 1), :])
            + jnp.where(first_lane, 0.0, pltpu.roll(value, 1, 1))
            + jnp.where(last_lane, 0.0, pltpu.roll(value, LANES - 1, 1))
        )

    def assemble(turn, change, k, c):
        p1, r1, kv1, qv1, diag1, res1 = c[:6]
        p, s, r, w = wet(k, turn, change)
        kv = r1 * r
        qv = kv * (p1 - p + 1.0)
        dg[block(k), :] = diag1 + kv1 + kv
        rs[block(k), :] = res1 + (qv - qv1)
        kvs[k] = kv
        sum1, sum2 = near(rp, k, r), near(wp, k, w)
        hr = 0.5 * r
        diag = 2.0 * s * (1.0 - s) + hr * sum1
        res = hr * (p * sum1 - sum2)
        if turn:
            res = res + 2.0 * (s - s0[k])
            return p, r, kv, qv, diag, res
        edge_rows(k, 0, p)
        edge_rows(k, 1, ks[k])
        acc = jnp.where(pair == k, pltpu.roll(p, 2 * k + 1, 1), c[6])
        acc = jnp.where(pair == k + HALF // 2, pltpu.roll(ks[k], HALF + 2 * k + 1, 1), acc)
        return p, r, kv, qv, diag, res, acc

    def finish(c):
        _, _, kv1, qv1, diag1, res1 = c[:6]
        dg[block(Z), :] = diag1 + kv1
        rs[block(Z), :] = res1 - qv1
        kvs[Z] = zero

    c_p.wait()
    c_k.wait()
    c = lax.fori_loop(0, Z, functools.partial(assemble, 0, None), (zero,) * 7, unroll=4)
    lsend[0] = c[6]
    finish(c)

    def halo(phase, row0, nrows):
        cs = [
            send(lsend.at[phase], lrecv.at[phase, 0], h_ssem.at[phase, 0], h_rsem.at[phase, 0], {"gy": right}),
            send(lsend.at[phase], lrecv.at[phase, 1], h_ssem.at[phase, 1], h_rsem.at[phase, 1], {"gy": left}),
            send(usend.at[pl.ds(row0, nrows)], urecv.at[pl.ds(row0, nrows)],
                 h_ssem.at[phase, 2], h_rsem.at[phase, 2], {"gx": up}),
            send(dsend.at[pl.ds(row0, nrows)], drecv.at[pl.ds(row0, nrows)],
                 h_ssem.at[phase, 3], h_rsem.at[phase, 3], {"gx": down}),
        ]
        sends.extend(cs)
        return cs

    h0 = halo(0, 0, 2)

    for c in o_copies:
        c.wait_recv()
    packed = pick_rows(orecv[...].reshape(rows, LANES)[:, :X], fields)
    for f in range(3):
        fsend[:, f, :, :] = packed[:, f * LANES:(f + 1) * LANES].reshape(GY, 8, LANES)[:, :SLOTS, :]
    f_copies = [
        send(fsend.at[peers[o]], frecv.at[gy], f_ssem.at[o], f_rsem.at[o], {"gy": peers[o]}) for o in offsets
    ]
    sends += f_copies
    frecv[gy] = fsend[gy]

    c_a.wait()
    c_v.wait()

    def moments(k, acc):
        a = age[k]
        m = var[k] + a * a
        ap[layer(k), :] = a
        mp[layer(k), :] = m
        mom[k] = m
        edge_rows(k, 2, a)
        edge_rows(k, 3, m)
        acc = jnp.where(pair == k, pltpu.roll(a, 2 * k + 1, 1), acc)
        return jnp.where(pair == k + HALF // 2, pltpu.roll(m, HALF + 2 * k + 1, 1), acc)

    lsend[1] = lax.fori_loop(0, Z, moments, zero, unroll=4)
    h1 = halo(1, 2, 2)

    def lane_halo(phase):
        return jnp.where(
            even, pltpu.roll(lrecv[phase, 1], LANES - 1, 1), pltpu.roll(lrecv[phase, 0], 1, 1)
        )

    for c in h0:
        c.wait_recv()
    lane_pk = lane_halo(0)
    inside = jnp.where(even, jnp.where(gy < GY - 1, 1.0, 0.0), jnp.where(gy > 0, 1.0, 0.0))
    above_in = jnp.where(gx > 0, 1.0, 0.0)
    below_in = jnp.where(gx < GX - 1, 1.0, 0.0)

    def compact_k(packed):
        return jnp.where(lane < HALF, pltpu.roll(packed, HALF, 1), 1.0)

    edge_k = (
        (compact_k(lane_pk), compact_k(lsend[0]), inside),
        (drecv[1], usend[1], above_in),
        (urecv[1], dsend[1], below_in),
    )

    def own_state(phase, n):
        return [
            (0.5 * root_conduct(sigmoid(op), ok), op)
            for (_, ok, _), op in zip(edge_k, (lsend[phase], usend[n], dsend[n]))
        ]

    def edge_state(phase, n, own):
        out = []
        for (hk, _, inner), hp, mine in zip(edge_k, (lane_halo(phase), drecv[n], urecv[n]), own):
            hr = root_conduct(sigmoid(hp), hk) * inner
            out.append((hr, hr * hp) + mine)
        return out

    def add_rows(ref, above, below):
        for row, value in ((0, above), (X - 1, below)):
            at = pl.ds(X + row, Z, stride=X)
            ref[at, :] = ref[at, :] + value

    def spread(k, compact):
        return jnp.where(edge, pltpu.roll(compact, LANES - 1 - 2 * k, 1), 0.0)

    def side_terms(phase, n, own):
        terms = [
            (half_r * hr, half_r * (own_p * hr - hw)) for hr, hw, half_r, own_p in edge_state(phase, n, own)
        ]
        add_rows(dg, terms[1][0], terms[2][0])
        add_rows(rs, terms[1][1], terms[2][1])
        return terms[0]

    def eliminate(k, coupling, inv, b, lanes):
        diag = dg[block(k + 1), :] + spread(k, lanes[0])
        res = rs[block(k + 1), :] + spread(k, lanes[1])
        g = coupling * inv
        b = g * b - res
        inv = 1.0 / (diag - coupling * g)
        yy[k] = b * inv
        return g, inv, b

    def from_below(lanes, k, c):
        g, inv, b = eliminate(k, kvs[k + 1], *c, lanes)
        gg[k + 1] = g
        return inv, b

    def update(k, n, d, acc):
        p = pc[k] + d
        pc[k] = p
        edge_rows(k, n, p)
        return jnp.where(pair == k, pltpu.roll(p, 2 * k + 1, 1), acc)

    lanes = side_terms(0, 0, own_state(0, 0))
    c = lax.fori_loop(0, Z - 1, lambda i, c: from_below(lanes, Z - 1 - i, c), (zero, zero), unroll=4)
    inv1[...] = c[0]
    c = from_below(lanes, 0, c)
    inv0 = c[0]
    d = yy[0]
    acc = update(0, 4, d, zero)
    slope[0] = zero
    usend[6, 0:1, :] = zero[0:1]
    dsend[6, 0:1, :] = zero[0:1]

    def downward(k, c):
        d, grow, acc, acc_g = c
        g = gg[k]
        d = yy[k] + g * d
        grow = jnp.where(k > 1, g * grow, grow)
        slope[k] = grow
        edge_rows(k, 6, grow)
        acc_g = jnp.where(pair == k, pltpu.roll(grow, 2 * k + 1, 1), acc_g)
        return d, grow, update(k, 4, d, acc), acc_g

    _, _, acc, acc_g = lax.fori_loop(1, Z, downward, (d, jnp.ones_like(zero), acc, zero), unroll=8)
    for f in f_copies:
        f.wait_recv()
    for f in range(3):
        tiles[f, :, :SLOTS, :] = frecv[:, f, :, :]
    got = pick_rows(take, jnp.concatenate([tiles[f].reshape(rows, LANES) for f in range(3)], axis=1))
    ext0 = got[:, :LANES] * s0[0]
    ext1 = got[:, LANES:2 * LANES] * s0[1]
    fall = got[:, 2 * LANES:]
    limit = ks[0] * (1.0 + 2.0 * (1.0 - s0[0]))
    infil = limit * fall / (limit + fall)
    d0 = -inv0 * (ext0 - infil + gg[1] * ext1)
    d1 = gg[1] * d0 - inv1[...] * ext1

    def ends(value):
        return jnp.where(
            even,
            jnp.broadcast_to(value[:, LANES - 1:], (X, LANES)),
            jnp.broadcast_to(value[:, :1], (X, LANES)),
        )

    lsend[2] = acc + acc_g * ends(d1) + jnp.where(pair == 0, ends(d0), 0.0)
    first = iota((Z, LANES), 0) == 0
    for ref, row in ((usend, 0), (dsend, X - 1)):
        d0_row, d1_row = (jnp.broadcast_to(v[row:row + 1], (Z, LANES)) for v in (d0, d1))
        ref[4] = ref[4] + ref[6] * d1_row + jnp.where(first, d0_row, 0.0)
    h2 = halo(2, 4, 1)

    pc[0] = pc[0] + d0
    c = lax.fori_loop(0, Z, functools.partial(assemble, 1, d1), (zero,) * 6, unroll=4)
    finish(c)
    rs[block(1), :] = rs[block(1), :] + (ext0 - infil)
    rs[block(2), :] = rs[block(2), :] + ext1
    own = own_state(2, 4)
    for c in h2:
        c.wait_recv()
    lanes = side_terms(2, 4, own)
    half = Z // 2

    def both_ends(i, c):
        inv_t, b_t, inv_b, b_b = c
        g, inv_t, b_t = eliminate(i, kvs[i], inv_t, b_t, lanes)
        gg[i] = g
        return (inv_t, b_t) + from_below(lanes, Z - 1 - i, (inv_b, b_b))

    inv_t, b_t, inv_b, b_b = lax.fori_loop(0, half, both_ends, (zero,) * 4, unroll=16)
    g = kvs[half] * inv_t
    d_b = (b_b + g * b_t) * inv_b / (1.0 - kvs[half] * g * inv_b)
    d_t = yy[half - 1] + g * d_b
    acc = update(half, 5, d_b, update(half - 1, 5, d_t, zero))

    def outward(i, c):
        d_t, d_b, acc = c
        t, b = half - 1 - i, half + i
        d_t = yy[t] + gg[t + 1] * d_t
        d_b = yy[b] + gg[b] * d_b
        return d_t, d_b, update(b, 5, d_b, update(t, 5, d_t, acc))

    lsend[3] = lax.fori_loop(1, half, outward, (d_t, d_b, acc), unroll=15)[2]
    h3 = halo(3, 5, 1)

    def flow(t, u, u_n, m, m_n):
        t_out, t_in = jnp.maximum(t, 0.0), jnp.minimum(t, 0.0)
        return t_out * u + t_in * u_n, t_out * m + t_in * m_n

    def outflows(k, c):
        p1, r1, a1, m1, ga1, gm1, out_a1, out_m1 = c
        p, s, r, w = wet(k, 1)
        a, m = ap[layer(k), :], mp[layer(k), :]
        ga, gm = flow(r1 * r * (p1 - p + 1.0), a1, a, m1, m)
        dg[block(k), :] = out_a1 + (ga - ga1)
        rs[block(k), :] = out_m1 + (gm - gm1)
        hr = 0.5 * r
        f_a, f_m = flow(
            jnp.where(last_lane, 0.0, pltpu.roll(r, LANES - 1, 1) * p - pltpu.roll(w, LANES - 1, 1)),
            a, pltpu.roll(a, LANES - 1, 1), m, pltpu.roll(m, LANES - 1, 1),
        )
        f_a, f_m = hr * f_a, hr * f_m
        u_a, u_m = flow(rp[layer(k, -1), :] * p - wp[layer(k, -1), :], a, ap[layer(k, -1), :], m, mp[layer(k, -1), :])
        d_a, d_m = flow(rp[layer(k, 1), :] * p - wp[layer(k, 1), :], a, ap[layer(k, 1), :], m, mp[layer(k, 1), :])
        out_a = hr * (u_a + d_a) + (f_a - pltpu.roll(f_a, 1, 1))
        out_m = hr * (u_m + d_m) + (f_m - pltpu.roll(f_m, 1, 1))
        return p, r, a, m, ga, gm, out_a, out_m

    c = lax.fori_loop(0, Z, outflows, (zero,) * 8, unroll=2)
    dg[block(Z), :] = c[6] - c[4]
    rs[block(Z), :] = c[7] - c[5]
    for k, ext in ((0, ext0), (1, ext1)):
        dg[block(k + 1), :] = dg[block(k + 1), :] + ext * ap[layer(k), :]
        rs[block(k + 1), :] = rs[block(k + 1), :] + ext * mp[layer(k), :]

    own = own_state(3, 5)
    for c in h1:
        c.wait_recv()
    lane_am = lane_halo(1)
    moment_edges = (
        (lane_am, lsend[1], pltpu.roll(lane_am, HALF, 1), pltpu.roll(lsend[1], HALF, 1)),
        (drecv[2], usend[2], drecv[3], usend[3]),
        (urecv[2], dsend[2], urecv[3], dsend[3]),
    )
    for c in sends[:-len(h3)]:
        c.wait_send()
    for c in h3:
        c.wait_recv()
    terms = []
    for (hr, hw, half_r, own_p), (ha, own_a, hm, own_m) in zip(edge_state(3, 5, own), moment_edges):
        f_a, f_m = flow(hr * own_p - hw, own_a, ha, own_m, hm)
        terms.append((half_r * f_a, half_r * f_m))
    add_rows(dg, terms[1][0], terms[2][0])
    add_rows(rs, terms[1][1], terms[2][1])

    terms_out[0] = terms[0][0]
    terms_out[1] = terms[0][1]
    for c in h3:
        c.wait_send()


def finale(
    Z, X, pc, landn, dg, rs, s0, sc, age, mom, terms, p_out, a_out, v_out, land_out, av, vv, out_sem
):
    copies = []

    def store(src, dst):
        c = pltpu.make_async_copy(src, dst, out_sem.at[len(copies)])
        c.start()
        copies.append(c)

    store(pc, p_out)
    store(landn, land_out)
    lane = iota((X, LANES), 1)
    edge = (lane == 0) | (lane == LANES - 1)

    def block(k):
        return pl.ds(pl.multiple_of(k * X, 8), X)

    def spread(k, compact):
        return jnp.where(edge, pltpu.roll(compact, LANES - 1 - 2 * k, 1), 0.0)

    def ages(k, _):
        a, m = age[k], mom[k]
        out_a = dg[block(k + 1), :] + spread(k, terms[0])
        out_m = rs[block(k + 1), :] + spread(k, terms[1])
        old = 0.05 + 0.4 * s0[k]
        inv = 1.0 / (0.05 + 0.4 * sc[k])
        a2 = (old * a - 0.2 * out_a) * inv + 0.2
        av[k] = a2
        vv[k] = (old * m - 0.2 * out_m) * inv + (0.4 - a2) * a2
        return 0

    chunk = Z // 4
    for n in range(4):
        lax.fori_loop(n * chunk, (n + 1) * chunk, ages, 0, unroll=8)
        at = pl.ds(n * chunk, chunk)
        store(av.at[at], a_out.at[at])
        store(vv.at[at], v_out.at[at])
    for c in copies:
        c.wait()


def shards(GX, GY, pressure, ksat, age_mean, age_var, remap, forcing, land_state, veg_class, veg_table):
    Z, X, _ = pressure.shape
    f32 = functools.partial(jax.ShapeDtypeStruct, dtype=F32)
    padded = pltpu.VMEM((Z * (X + 2 * PAD), LANES), F32)
    flat = pltpu.VMEM(((Z + 1) * X, LANES), F32)
    plain = pltpu.VMEM((Z + 1, X, LANES), F32)
    land = pltpu.VMEM(land_state.shape, F32)
    exact = pltpu.VMEM((Z, X, LANES), F32)
    dma = pltpu.SemaphoreType.DMA
    any_spec = pl.BlockSpec(memory_space=pl.ANY)
    vmem_spec = pl.BlockSpec(memory_space=pltpu.VMEM)
    inputs = (pressure, ksat, age_mean, age_var, remap.reshape(1, X), forcing, land_state, veg_class, veg_table)
    held = pl.pallas_call(
        functools.partial(kernel, Z, X, GX, GY),
        out_shape=(exact, land, flat, flat, exact, exact, exact, exact, pltpu.VMEM((2, X, LANES), F32)),
        in_specs=[any_spec] * 9,
        out_specs=(vmem_spec,) * 9,
        scratch_shapes=[padded] * 4 + [exact] + [plain] * 3 + [exact] * 2 + [pltpu.VMEM((X, LANES), F32)] + [
            pltpu.VMEM((1, X), jnp.int32),
            pltpu.VMEM(forcing.shape, F32),
            pltpu.VMEM(land_state.shape, F32),
            pltpu.VMEM(veg_class.shape, jnp.int32),
            pltpu.SMEM(veg_table.shape, F32),
            pltpu.VMEM((GY, 8, LANES), F32),
            pltpu.VMEM((GY, 8, LANES), F32),
            pltpu.VMEM((GY, 3, SLOTS, LANES), F32),
            pltpu.VMEM((GY, 3, SLOTS, LANES), F32),
            pltpu.VMEM((3, GY, 8, LANES), F32),
            pltpu.VMEM((4, X, LANES), F32),
            pltpu.VMEM((4, 2, X, LANES), F32),
            pltpu.VMEM((7, Z, LANES), F32),
            pltpu.VMEM((6, Z, LANES), F32),
            pltpu.VMEM((7, Z, LANES), F32),
            pltpu.VMEM((6, Z, LANES), F32),
            dma((9,)), dma((GY,)), dma((GY,)), dma((GY,)), dma((GY,)), dma((4, 4)), dma((4, 4)),
        ],
        compiler_params=pltpu.CompilerParams(
            collective_id=0, has_side_effects=True, vmem_limit_bytes=24 * 1024 * 1024
        ),
    )(*(pltpu.with_memory_space_constraint(x, pltpu.HBM) for x in inputs))
    return pl.pallas_call(
        functools.partial(finale, Z, X),
        out_shape=(
            f32((Z, X, LANES)), f32((Z, X, LANES)), f32((Z, X, LANES)), f32(land_state.shape),
        ),
        in_specs=[vmem_spec] * 9,
        out_specs=(any_spec,) * 4,
        scratch_shapes=[exact, exact, dma((10,))],
        compiler_params=pltpu.CompilerParams(vmem_limit_bytes=8 * 1024 * 1024),
    )(*held)


def solution(mesh):
    field = P(None, "gx", "gy")
    return jax.shard_map(
        functools.partial(shards, mesh.shape["gx"], mesh.shape["gy"]),
        mesh=mesh,
        in_specs=(field, field, field, field, P("gx", "gy"), field, field, P("gx", "gy"), P()),
        out_specs=(field, field, field, field),
        check_vma=False,
    )
```

```python
import functools
import math

import jax
import jax.numpy as jnp
from jax import lax
from jax.experimental import pallas as pl
from jax.experimental.pallas import tpu as pltpu
from jax.sharding import PartitionSpec as P

LANES = 128
HALF = 64
PAD = 8
SLOTS = 4
FAR = 1
F32 = jnp.float32
BF16 = jnp.bfloat16
MESH = pl.DeviceIdType.MESH


def sigmoid(x):
    return 0.5 * jnp.tanh(0.5 * x) + 0.5


def root_conduct(s, ksat):
    x = ksat * (0.05 + s * s)
    return x * lax.rsqrt(x)


def iota(shape, dim):
    return lax.broadcasted_iota(jnp.int32, shape, dim)


def pieces(x):
    high = x.astype(BF16)
    rest = x - high.astype(F32)
    mid = rest.astype(BF16)
    return high, mid, (rest - mid.astype(F32)).astype(BF16)


def pick_rows(one_hot, x):
    n = x.shape[1]
    out = jnp.dot(one_hot.astype(BF16), jnp.concatenate(pieces(x), axis=1), preferred_element_type=F32)
    return (out[:, 2 * n:] + out[:, n:2 * n]) + out[:, :n]


def kernel(
    Z, X, GX, GY,
    p_hbm, k_hbm, a_hbm, v_hbm, remap_hbm, forc_hbm, state_hbm, veg_hbm, table_hbm,
    pc, landn, dg, rs, s0, sc, age, mom, terms_out,
    rp, wp, ap, mp, ks, gg, yy, kvs, var, slope, inv1,
    remap, forc, state, veg, table,
    osend, orecv, fsend, frecv, tiles, bsend, brecv,
    lsend, lrecv, usend, urecv, dsend, drecv,
    load_sem, o_ssem, o_rsem, f_ssem, f_rsem, h_ssem, h_rsem, w_ssem, w_rsem,
):
    gx, gy = lax.axis_index("gx"), lax.axis_index("gy")
    up, down = lax.rem(gx + GX - 1, GX), lax.rem(gx + 1, GX)
    left, right = lax.rem(gy + GY - 1, GY), lax.rem(gy + 1, GY)
    stride = X + 2 * PAD
    side = math.isqrt(GY)

    def layer(k, shift=0):
        return pl.ds(pl.multiple_of(k * stride, 8) + (PAD + shift), X)

    def block(k):
        return pl.ds(pl.multiple_of(k * X, 8), X)

    def far(o):
        dy, dx = o // side, o % side
        return min(dy, side - dy) + min(dx, side - dx)

    offsets = sorted(range(1, GY), key=lambda o: -far(o))
    my_y, my_x = gy // side, lax.rem(gy, side)
    whole, packed_to = offsets[:FAR], offsets[FAR:]
    peers = {
        o: lax.rem(my_y + o // side, side) * side + lax.rem(my_x + o % side, side) for o in offsets
    }

    def load(src, dst, n):
        c = pltpu.make_async_copy(src, dst, load_sem.at[n])
        c.start()
        return c

    barrier = pltpu.get_barrier_semaphore()
    for o in offsets:
        pl.semaphore_signal(barrier, inc=1, device_id={"gy": peers[o]}, device_id_type=MESH)
    for d in (up, down):
        pl.semaphore_signal(barrier, inc=1, device_id={"gx": d}, device_id_type=MESH)
    c_remap = load(remap_hbm, remap, 0)
    c_forc = load(forc_hbm, forc, 3)
    c_state = load(state_hbm, state, 4)
    c_veg = load(veg_hbm, veg, 5)
    c_table = load(table_hbm, table, 6)
    c_p = load(p_hbm, pc, 1)
    c_k = load(k_hbm, ks, 2)
    c_a = load(a_hbm, age, 7)
    c_v = load(v_hbm, var, 8)

    def send(src, dst, ssem, rsem, where):
        c = pltpu.make_async_remote_copy(
            src_ref=src, dst_ref=dst, send_sem=ssem, recv_sem=rsem,
            device_id=where, device_id_type=MESH,
        )
        c.start()
        return c

    lane = iota((X, LANES), 1)
    pair = lane >> 1
    first_lane, last_lane = lane == 0, lane == LANES - 1
    edge = first_lane | last_lane
    even = (lane & 1) == 0
    zero = jnp.zeros((X, LANES), F32)
    pad = jnp.zeros((PAD, LANES), F32)

    c_remap.wait()
    bits = X.bit_length() - 1
    code_row = remap[...]
    eye = iota((X, X), 0) == iota((X, X), 1)
    code_col = jnp.sum(jnp.where(eye, jnp.broadcast_to(code_row, (X, X)), 0), axis=1, keepdims=True)
    dest_row, dest_col = code_row >> bits, code_col >> bits
    slot_col = code_col & (X - 1)
    same = jnp.broadcast_to(dest_col, (X, X)) == jnp.broadcast_to(dest_row, (X, X))
    rank_row = jnp.sum(jnp.where(same & (iota((X, X), 0) < iota((X, X), 1)), 1, 0), axis=0, keepdims=True)
    rank_col = jnp.sum(jnp.where(same & (iota((X, X), 1) < iota((X, X), 0)), 1, 0), axis=1, keepdims=True)
    rows = 8 * GY
    row_id = iota((rows, X), 0)
    row_key = (row_id >> 3) * SLOTS + (row_id & (SLOTS - 1))
    tile_of_row = (row_key == jnp.broadcast_to(dest_row * SLOTS + rank_row, (rows, X))).astype(BF16)
    slot_of_tile = (jnp.broadcast_to(slot_col, (X, LANES)) == iota((X, LANES), 1)).astype(BF16)
    osend[...] = jnp.dot(tile_of_row, slot_of_tile, preferred_element_type=F32).reshape(GY, 8, LANES)

    pl.semaphore_wait(barrier, GY + 1)

    sends = []
    o_copies = [
        send(osend.at[peers[o]], orecv.at[gy], o_ssem.at[o], o_rsem.at[o], {"gy": peers[o]}) for o in packed_to
    ]
    sends += o_copies
    orecv[gy] = osend[gy]
    for o in whole:
        sender = side * lax.rem(my_y + side - o // side, side) + lax.rem(my_x + side - o % side, side)
        orecv[sender] = jnp.zeros((8, LANES), F32)
        frecv[sender] = jnp.zeros((3, SLOTS, LANES), F32)

    row_of_tile = jnp.broadcast_to(dest_col * 8 + rank_col, (X, rows))
    take = [(row_of_tile == iota((X, rows), 1)).astype(F32)]
    for o in whole:
        sender = side * lax.rem(my_y + side - o // side, side) + lax.rem(my_x + side - o % side, side)
        here = (dest_col == sender) & (slot_col == iota((X, X), 1))
        take.append(here.astype(F32))
    take = jnp.concatenate(take, axis=1)
    tiles[...] = jnp.zeros_like(tiles)

    c_veg.wait()
    c_table.wait()
    c_forc.wait()
    c_state.wait()
    cls = veg[...]
    nveg = table.shape[1]
    par = [jnp.full((X, LANES), table[i, 0], F32) for i in range(5)]
    for v in range(1, nveg):
        hit = cls == v
        par = [jnp.where(hit, table[i, v], par[i]) for i in range(5)]
    albedo, conduct, capacity, et_factor, decay = par
    skin = (state[0] + 0.5 * ((1.0 - albedo) * 2.0 * forc[0] + 0.5 * forc[1] + forc[2])) / 1.5
    soft = jnp.maximum(skin, 0.0) + jnp.log(1.0 + jnp.exp(-jnp.abs(skin)))
    demand = conduct * soft * (1.0 + forc[4]) * (1.0 - 0.5 * forc[3]) / (0.5 + forc[5])
    wetted = state[1] + forc[6]
    drip = jnp.maximum(wetted - capacity, 0.0)
    canopy = (wetted - drip) * capacity / (demand + capacity)
    through = drip + 0.5 * forc[6]
    draw0 = 0.5 * et_factor * demand / (1.0 + decay)
    draw1 = draw0 * decay
    landn[0] = skin
    landn[1] = canopy
    fields = jnp.concatenate([draw0, draw1, through], axis=1)
    for f, part in enumerate((draw0, draw1, through)):
        bsend[f] = part
    w_copies = [
        send(bsend, brecv.at[n], w_ssem.at[n], w_rsem.at[n], {"gy": peers[o]}) for n, o in enumerate(whole)
    ]
    sends += w_copies

    for ref in (rp, wp, ap, mp):
        for k in range(Z):
            ref[k * stride:k * stride + PAD, :] = pad
            ref[k * stride + PAD + X:(k + 1) * stride, :] = pad

    def edge_rows(k, n, value):
        usend[n, pl.ds(k, 1), :] = value[0:1]
        dsend[n, pl.ds(k, 1), :] = value[X - 1:X]

    def wet(k, turn, change=None):
        p = pc[k]
        if change is not None:
            p = p + slope[k] * change
            pc[k] = p
        s = sigmoid(p)
        r = root_conduct(s, ks[k])
        w = r * p
        (sc if turn else s0)[k] = s
        rp[layer(k), :] = r
        wp[layer(k), :] = w
        return p, s, r, w

    def near(ref, k, value):
        return (
            (ref[layer(k, -1), :] + ref[layer(k, 1), :])
            + jnp.where(first_lane, 0.0, pltpu.roll(value, 1, 1))
            + jnp.where(last_lane, 0.0, pltpu.roll(value, LANES - 1, 1))
        )

    def assemble(turn, change, k, c):
        p1, r1, kv1, qv1, diag1, res1 = c[:6]
        p, s, r, w = wet(k, turn, change)
        kv = r1 * r
        qv = kv * (p1 - p + 1.0)
        dg[block(k), :] = diag1 + kv1 + kv
        rs[block(k), :] = res1 + (qv - qv1)
        kvs[k] = kv
        sum1, sum2 = near(rp, k, r), near(wp, k, w)
        hr = 0.5 * r
        diag = 2.0 * s * (1.0 - s) + hr * sum1
        res = hr * (p * sum1 - sum2)
        if turn:
            res = res + 2.0 * (s - s0[k])
            return p, r, kv, qv, diag, res
        edge_rows(k, 0, p)
        edge_rows(k, 1, ks[k])
        acc = jnp.where(pair == k, pltpu.roll(p, 2 * k + 1, 1), c[6])
        acc = jnp.where(pair == k + HALF // 2, pltpu.roll(ks[k], HALF + 2 * k + 1, 1), acc)
        return p, r, kv, qv, diag, res, acc

    def finish(c):
        _, _, kv1, qv1, diag1, res1 = c[:6]
        dg[block(Z), :] = diag1 + kv1
        rs[block(Z), :] = res1 - qv1
        kvs[Z] = zero

    c_p.wait()
    c_k.wait()
    c = lax.fori_loop(0, Z, functools.partial(assemble, 0, None), (zero,) * 7, unroll=4)
    lsend[0] = c[6]
    finish(c)

    def halo(phase, row0, nrows):
        cs = [
            send(lsend.at[phase], lrecv.at[phase, 0], h_ssem.at[phase, 0], h_rsem.at[phase, 0], {"gy": right}),
            send(lsend.at[phase], lrecv.at[phase, 1], h_ssem.at[phase, 1], h_rsem.at[phase, 1], {"gy": left}),
            send(usend.at[pl.ds(row0, nrows)], urecv.at[pl.ds(row0, nrows)],
                 h_ssem.at[phase, 2], h_rsem.at[phase, 2], {"gx": up}),
            send(dsend.at[pl.ds(row0, nrows)], drecv.at[pl.ds(row0, nrows)],
                 h_ssem.at[phase, 3], h_rsem.at[phase, 3], {"gx": down}),
        ]
        sends.extend(cs)
        return cs

    h0 = halo(0, 0, 2)

    for c in o_copies:
        c.wait_recv()
    packed = pick_rows(orecv[...].reshape(rows, LANES)[:, :X], fields)
    for f in range(3):
        fsend[:, f, :, :] = packed[:, f * LANES:(f + 1) * LANES].reshape(GY, 8, LANES)[:, :SLOTS, :]
    f_copies = [
        send(fsend.at[peers[o]], frecv.at[gy], f_ssem.at[o], f_rsem.at[o], {"gy": peers[o]}) for o in packed_to
    ]
    sends += f_copies
    frecv[gy] = fsend[gy]

    c_a.wait()
    c_v.wait()

    def moments(k, acc):
        a = age[k]
        m = var[k] + a * a
        ap[layer(k), :] = a
        mp[layer(k), :] = m
        mom[k] = m
        edge_rows(k, 2, a)
        edge_rows(k, 3, m)
        acc = jnp.where(pair == k, pltpu.roll(a, 2 * k + 1, 1), acc)
        return jnp.where(pair == k + HALF // 2, pltpu.roll(m, HALF + 2 * k + 1, 1), acc)

    lsend[1] = lax.fori_loop(0, Z, moments, zero, unroll=4)
    h1 = halo(1, 2, 2)

    def lane_halo(phase):
        return jnp.where(
            even, pltpu.roll(lrecv[phase, 1], LANES - 1, 1), pltpu.roll(lrecv[phase, 0], 1, 1)
        )

    for c in h0:
        c.wait_recv()
    lane_pk = lane_halo(0)
    inside = jnp.where(even, jnp.where(gy < GY - 1, 1.0, 0.0), jnp.where(gy > 0, 1.0, 0.0))
    above_in = jnp.where(gx > 0, 1.0, 0.0)
    below_in = jnp.where(gx < GX - 1, 1.0, 0.0)

    def compact_k(packed):
        return jnp.where(lane < HALF, pltpu.roll(packed, HALF, 1), 1.0)

    edge_k = (
        (compact_k(lane_pk), compact_k(lsend[0]), inside),
        (drecv[1], usend[1], above_in),
        (urecv[1], dsend[1], below_in),
    )

    def own_state(phase, n):
        return [
            (0.5 * root_conduct(sigmoid(op), ok), op)
            for (_, ok, _), op in zip(edge_k, (lsend[phase], usend[n], dsend[n]))
        ]

    def edge_state(phase, n, own):
        out = []
        for (hk, _, inner), hp, mine in zip(edge_k, (lane_halo(phase), drecv[n], urecv[n]), own):
            hr = root_conduct(sigmoid(hp), hk) * inner
            out.append((hr, hr * hp) + mine)
        return out

    def add_rows(ref, above, below):
        for row, value in ((0, above), (X - 1, below)):
            at = pl.ds(X + row, Z, stride=X)
            ref[at, :] = ref[at, :] + value

    def spread(k, compact):
        return jnp.where(edge, pltpu.roll(compact, LANES - 1 - 2 * k, 1), 0.0)

    def side_terms(phase, n, own):
        terms = [
            (half_r * hr, half_r * (own_p * hr - hw)) for hr, hw, half_r, own_p in edge_state(phase, n, own)
        ]
        add_rows(dg, terms[1][0], terms[2][0])
        add_rows(rs, terms[1][1], terms[2][1])
        return terms[0]

    def eliminate(k, coupling, inv, b, lanes):
        diag = dg[block(k + 1), :] + spread(k, lanes[0])
        res = rs[block(k + 1), :] + spread(k, lanes[1])
        g = coupling * inv
        b = g * b - res
        inv = 1.0 / (diag - coupling * g)
        yy[k] = b * inv
        return g, inv, b

    def from_below(lanes, k, c):
        g, inv, b = eliminate(k, kvs[k + 1], *c, lanes)
        gg[k + 1] = g
        return inv, b

    def update(k, n, d, acc):
        p = pc[k] + d
        pc[k] = p
        edge_rows(k, n, p)
        return jnp.where(pair == k, pltpu.roll(p, 2 * k + 1, 1), acc)

    lanes = side_terms(0, 0, own_state(0, 0))
    c = lax.fori_loop(0, Z - 1, lambda i, c: from_below(lanes, Z - 1 - i, c), (zero, zero), unroll=4)
    inv1[...] = c[0]
    c = from_below(lanes, 0, c)
    inv0 = c[0]
    d = yy[0]
    acc = update(0, 4, d, zero)
    slope[0] = zero
    usend[6, 0:1, :] = zero[0:1]
    dsend[6, 0:1, :] = zero[0:1]

    def downward(k, c):
        d, grow, acc, acc_g = c
        g = gg[k]
        d = yy[k] + g * d
        grow = jnp.where(k > 1, g * grow, grow)
        slope[k] = grow
        edge_rows(k, 6, grow)
        acc_g = jnp.where(pair == k, pltpu.roll(grow, 2 * k + 1, 1), acc_g)
        return d, grow, update(k, 4, d, acc), acc_g

    _, _, acc, acc_g = lax.fori_loop(1, Z, downward, (d, jnp.ones_like(zero), acc, zero), unroll=8)
    for f in w_copies + f_copies:
        f.wait_recv()
    for f in range(3):
        tiles[f, :, :SLOTS, :] = frecv[:, f, :, :]
    given = [jnp.concatenate([tiles[f].reshape(rows, LANES) for f in range(3)], axis=1)]
    for n in range(FAR):
        given.append(jnp.concatenate([brecv[n, f] for f in range(3)], axis=1))
    got = pick_rows(take, jnp.concatenate(given, axis=0))
    ext0 = got[:, :LANES] * s0[0]
    ext1 = got[:, LANES:2 * LANES] * s0[1]
    fall = got[:, 2 * LANES:]
    limit = ks[0] * (1.0 + 2.0 * (1.0 - s0[0]))
    infil = limit * fall / (limit + fall)
    d0 = -inv0 * (ext0 - infil + gg[1] * ext1)
    d1 = gg[1] * d0 - inv1[...] * ext1

    def ends(value):
        return jnp.where(
            even,
            jnp.broadcast_to(value[:, LANES - 1:], (X, LANES)),
            jnp.broadcast_to(value[:, :1], (X, LANES)),
        )

    lsend[2] = acc + acc_g * ends(d1) + jnp.where(pair == 0, ends(d0), 0.0)
    first = iota((Z, LANES), 0) == 0
    for ref, row in ((usend, 0), (dsend, X - 1)):
        d0_row, d1_row = (jnp.broadcast_to(v[row:row + 1], (Z, LANES)) for v in (d0, d1))
        ref[4] = ref[4] + ref[6] * d1_row + jnp.where(first, d0_row, 0.0)
    h2 = halo(2, 4, 1)

    pc[0] = pc[0] + d0
    c = lax.fori_loop(0, Z, functools.partial(assemble, 1, d1), (zero,) * 6, unroll=4)
    finish(c)
    rs[block(1), :] = rs[block(1), :] + (ext0 - infil)
    rs[block(2), :] = rs[block(2), :] + ext1
    own = own_state(2, 4)
    for c in h2:
        c.wait_recv()
    lanes = side_terms(2, 4, own)
    half = Z // 2

    def both_ends(i, c):
        inv_t, b_t, inv_b, b_b = c
        g, inv_t, b_t = eliminate(i, kvs[i], inv_t, b_t, lanes)
        gg[i] = g
        return (inv_t, b_t) + from_below(lanes, Z - 1 - i, (inv_b, b_b))

    inv_t, b_t, inv_b, b_b = lax.fori_loop(0, half, both_ends, (zero,) * 4, unroll=16)
    g = kvs[half] * inv_t
    d_b = (b_b + g * b_t) * inv_b / (1.0 - kvs[half] * g * inv_b)
    d_t = yy[half - 1] + g * d_b
    acc = update(half, 5, d_b, update(half - 1, 5, d_t, zero))

    def outward(i, c):
        d_t, d_b, acc = c
        t, b = half - 1 - i, half + i
        d_t = yy[t] + gg[t + 1] * d_t
        d_b = yy[b] + gg[b] * d_b
        return d_t, d_b, update(b, 5, d_b, update(t, 5, d_t, acc))

    lsend[3] = lax.fori_loop(1, half, outward, (d_t, d_b, acc), unroll=15)[2]
    h3 = halo(3, 5, 1)

    def flow(t, u, u_n, m, m_n):
        t_out, t_in = jnp.maximum(t, 0.0), jnp.minimum(t, 0.0)
        return t_out * u + t_in * u_n, t_out * m + t_in * m_n

    def outflows(k, c):
        p1, r1, a1, m1, ga1, gm1, out_a1, out_m1 = c
        p, s, r, w = wet(k, 1)
        a, m = ap[layer(k), :], mp[layer(k), :]
        ga, gm = flow(r1 * r * (p1 - p + 1.0), a1, a, m1, m)
        dg[block(k), :] = out_a1 + (ga - ga1)
        rs[block(k), :] = out_m1 + (gm - gm1)
        hr = 0.5 * r
        f_a, f_m = flow(
            jnp.where(last_lane, 0.0, pltpu.roll(r, LANES - 1, 1) * p - pltpu.roll(w, LANES - 1, 1)),
            a, pltpu.roll(a, LANES - 1, 1), m, pltpu.roll(m, LANES - 1, 1),
        )
        f_a, f_m = hr * f_a, hr * f_m
        u_a, u_m = flow(rp[layer(k, -1), :] * p - wp[layer(k, -1), :], a, ap[layer(k, -1), :], m, mp[layer(k, -1), :])
        d_a, d_m = flow(rp[layer(k, 1), :] * p - wp[layer(k, 1), :], a, ap[layer(k, 1), :], m, mp[layer(k, 1), :])
        out_a = hr * (u_a + d_a) + (f_a - pltpu.roll(f_a, 1, 1))
        out_m = hr * (u_m + d_m) + (f_m - pltpu.roll(f_m, 1, 1))
        return p, r, a, m, ga, gm, out_a, out_m

    c = lax.fori_loop(0, Z, outflows, (zero,) * 8, unroll=2)
    dg[block(Z), :] = c[6] - c[4]
    rs[block(Z), :] = c[7] - c[5]
    for k, ext in ((0, ext0), (1, ext1)):
        dg[block(k + 1), :] = dg[block(k + 1), :] + ext * ap[layer(k), :]
        rs[block(k + 1), :] = rs[block(k + 1), :] + ext * mp[layer(k), :]

    own = own_state(3, 5)
    for c in h1:
        c.wait_recv()
    lane_am = lane_halo(1)
    moment_edges = (
        (lane_am, lsend[1], pltpu.roll(lane_am, HALF, 1), pltpu.roll(lsend[1], HALF, 1)),
        (drecv[2], usend[2], drecv[3], usend[3]),
        (urecv[2], dsend[2], urecv[3], dsend[3]),
    )
    for c in sends[:-len(h3)]:
        c.wait_send()
    for c in h3:
        c.wait_recv()
    terms = []
    for (hr, hw, half_r, own_p), (ha, own_a, hm, own_m) in zip(edge_state(3, 5, own), moment_edges):
        f_a, f_m = flow(hr * own_p - hw, own_a, ha, own_m, hm)
        terms.append((half_r * f_a, half_r * f_m))
    add_rows(dg, terms[1][0], terms[2][0])
    add_rows(rs, terms[1][1], terms[2][1])

    terms_out[0] = terms[0][0]
    terms_out[1] = terms[0][1]
    for c in h3:
        c.wait_send()


def finale(
    Z, X, pc, landn, dg, rs, s0, sc, age, mom, terms, p_out, a_out, v_out, land_out, av, vv, out_sem
):
    copies = []

    def store(src, dst):
        c = pltpu.make_async_copy(src, dst, out_sem.at[len(copies)])
        c.start()
        copies.append(c)

    store(pc, p_out)
    store(landn, land_out)
    lane = iota((X, LANES), 1)
    edge = (lane == 0) | (lane == LANES - 1)

    def block(k):
        return pl.ds(pl.multiple_of(k * X, 8), X)

    def spread(k, compact):
        return jnp.where(edge, pltpu.roll(compact, LANES - 1 - 2 * k, 1), 0.0)

    def ages(k, _):
        a, m = age[k], mom[k]
        out_a = dg[block(k + 1), :] + spread(k, terms[0])
        out_m = rs[block(k + 1), :] + spread(k, terms[1])
        old = 0.05 + 0.4 * s0[k]
        inv = 1.0 / (0.05 + 0.4 * sc[k])
        a2 = (old * a - 0.2 * out_a) * inv + 0.2
        av[k] = a2
        vv[k] = (old * m - 0.2 * out_m) * inv + (0.4 - a2) * a2
        return 0

    chunk = Z // 4
    for n in range(4):
        lax.fori_loop(n * chunk, (n + 1) * chunk, ages, 0, unroll=8)
        at = pl.ds(n * chunk, chunk)
        store(av.at[at], a_out.at[at])
        store(vv.at[at], v_out.at[at])
    for c in copies:
        c.wait()


def shards(GX, GY, pressure, ksat, age_mean, age_var, remap, forcing, land_state, veg_class, veg_table):
    Z, X, _ = pressure.shape
    f32 = functools.partial(jax.ShapeDtypeStruct, dtype=F32)
    padded = pltpu.VMEM((Z * (X + 2 * PAD), LANES), F32)
    flat = pltpu.VMEM(((Z + 1) * X, LANES), F32)
    plain = pltpu.VMEM((Z + 1, X, LANES), F32)
    land = pltpu.VMEM(land_state.shape, F32)
    exact = pltpu.VMEM((Z, X, LANES), F32)
    dma = pltpu.SemaphoreType.DMA
    any_spec = pl.BlockSpec(memory_space=pl.ANY)
    vmem_spec = pl.BlockSpec(memory_space=pltpu.VMEM)
    inputs = (pressure, ksat, age_mean, age_var, remap.reshape(1, X), forcing, land_state, veg_class, veg_table)
    held = pl.pallas_call(
        functools.partial(kernel, Z, X, GX, GY),
        out_shape=(exact, land, flat, flat, exact, exact, exact, exact, pltpu.VMEM((2, X, LANES), F32)),
        in_specs=[any_spec] * 9,
        out_specs=(vmem_spec,) * 9,
        scratch_shapes=[padded] * 4 + [exact] + [plain] * 3 + [exact] * 2 + [pltpu.VMEM((X, LANES), F32)] + [
            pltpu.VMEM((1, X), jnp.int32),
            pltpu.VMEM(forcing.shape, F32),
            pltpu.VMEM(land_state.shape, F32),
            pltpu.VMEM(veg_class.shape, jnp.int32),
            pltpu.SMEM(veg_table.shape, F32),
            pltpu.VMEM((GY, 8, LANES), F32),
            pltpu.VMEM((GY, 8, LANES), F32),
            pltpu.VMEM((GY, 3, SLOTS, LANES), F32),
            pltpu.VMEM((GY, 3, SLOTS, LANES), F32),
            pltpu.VMEM((3, GY, 8, LANES), F32),
            pltpu.VMEM((3, X, LANES), F32),
            pltpu.VMEM((FAR, 3, X, LANES), F32),
            pltpu.VMEM((4, X, LANES), F32),
            pltpu.VMEM((4, 2, X, LANES), F32),
            pltpu.VMEM((7, Z, LANES), F32),
            pltpu.VMEM((6, Z, LANES), F32),
            pltpu.VMEM((7, Z, LANES), F32),
            pltpu.VMEM((6, Z, LANES), F32),
            dma((9,)), dma((GY,)), dma((GY,)), dma((GY,)), dma((GY,)), dma((4, 4)), dma((4, 4)), dma((FAR,)), dma((FAR,)),
        ],
        compiler_params=pltpu.CompilerParams(
            collective_id=0, has_side_effects=True, vmem_limit_bytes=24 * 1024 * 1024
        ),
    )(*(pltpu.with_memory_space_constraint(x, pltpu.HBM) for x in inputs))
    return pl.pallas_call(
        functools.partial(finale, Z, X),
        out_shape=(
            f32((Z, X, LANES)), f32((Z, X, LANES)), f32((Z, X, LANES)), f32(land_state.shape),
        ),
        in_specs=[vmem_spec] * 9,
        out_specs=(any_spec,) * 4,
        scratch_shapes=[exact, exact, dma((10,))],
        compiler_params=pltpu.CompilerParams(vmem_limit_bytes=8 * 1024 * 1024),
    )(*held)


def solution(mesh):
    field = P(None, "gx", "gy")
    return jax.shard_map(
        functools.partial(shards, mesh.shape["gx"], mesh.shape["gy"]),
        mesh=mesh,
        in_specs=(field, field, field, field, P("gx", "gy"), field, field, P("gx", "gy"), P()),
        out_specs=(field, field, field, field),
        check_vma=False,
    )
```

```python
import functools
import math

import jax
import jax.numpy as jnp
from jax import lax
from jax.experimental import pallas as pl
from jax.experimental.pallas import tpu as pltpu
from jax.sharding import PartitionSpec as P

LANES = 128
HALF = 64
PAD = 8
SLOTS = 4
FAR = 1
F32 = jnp.float32
BF16 = jnp.bfloat16
MESH = pl.DeviceIdType.MESH


def sigmoid(x):
    return 0.5 * jnp.tanh(0.5 * x) + 0.5


def root_conduct(s, ksat):
    x = ksat * (0.05 + s * s)
    return x * lax.rsqrt(x)


def iota(shape, dim):
    return lax.broadcasted_iota(jnp.int32, shape, dim)


def pieces(x):
    high = x.astype(BF16)
    rest = x - high.astype(F32)
    mid = rest.astype(BF16)
    return high, mid, (rest - mid.astype(F32)).astype(BF16)


def pick_rows(one_hot, x):
    n = x.shape[1]
    out = jnp.dot(one_hot.astype(BF16), jnp.concatenate(pieces(x), axis=1), preferred_element_type=F32)
    return (out[:, 2 * n:] + out[:, n:2 * n]) + out[:, :n]


def kernel(
    Z, X, GX, GY,
    p_hbm, k_hbm, a_hbm, v_hbm, remap_hbm, forc_hbm, state_hbm, veg_hbm, table_hbm,
    pc, landn, dg, rs, s0, sc, age, mom, terms_out,
    rp, wp, ap, mp, ks, gg, yy, kvs, var, slope, inv1,
    remap, forc, state, veg, table,
    osend, orecv, fsend, frecv, tiles, bsend, brecv,
    lsend, lrecv, usend, urecv, dsend, drecv,
    load_sem, o_ssem, o_rsem, f_ssem, f_rsem, h_ssem, h_rsem, w_ssem, w_rsem,
):
    gx, gy = lax.axis_index("gx"), lax.axis_index("gy")
    up, down = lax.rem(gx + GX - 1, GX), lax.rem(gx + 1, GX)
    left, right = lax.rem(gy + GY - 1, GY), lax.rem(gy + 1, GY)
    stride = X + 2 * PAD
    mid = X // 2
    side = math.isqrt(GY)

    def layer(k, shift=0):
        return pl.ds(pl.multiple_of(k * stride, 8) + (PAD + shift), X)

    def block(k):
        return pl.ds(pl.multiple_of(k * X, 8), X)

    def far(o):
        dy, dx = o // side, o % side
        return min(dy, side - dy) + min(dx, side - dx)

    offsets = sorted(range(1, GY), key=lambda o: -far(o))
    my_y, my_x = gy // side, lax.rem(gy, side)
    whole, packed_to = offsets[:FAR], offsets[FAR:]
    peers = {
        o: lax.rem(my_y + o // side, side) * side + lax.rem(my_x + o % side, side) for o in offsets
    }

    def load(src, dst, n):
        c = pltpu.make_async_copy(src, dst, load_sem.at[n])
        c.start()
        return c

    barrier = pltpu.get_barrier_semaphore()
    for o in offsets:
        pl.semaphore_signal(barrier, inc=1, device_id={"gy": peers[o]}, device_id_type=MESH)
    for d in (up, down):
        pl.semaphore_signal(barrier, inc=1, device_id={"gx": d}, device_id_type=MESH)
    c_remap = load(remap_hbm, remap, 0)
    c_forc = load(forc_hbm, forc, 3)
    c_state = load(state_hbm, state, 4)
    c_veg = load(veg_hbm, veg, 5)
    c_table = load(table_hbm, table, 6)
    c_p = load(p_hbm, pc, 1)
    c_k = load(k_hbm, ks, 2)
    c_a = load(a_hbm, age, 7)
    c_v = load(v_hbm, var, 8)

    def send(src, dst, ssem, rsem, where):
        c = pltpu.make_async_remote_copy(
            src_ref=src, dst_ref=dst, send_sem=ssem, recv_sem=rsem,
            device_id=where, device_id_type=MESH,
        )
        c.start()
        return c

    lane = iota((X, LANES), 1)
    pair = lane >> 1
    first_lane, last_lane = lane == 0, lane == LANES - 1
    edge = first_lane | last_lane
    even = (lane & 1) == 0
    zero = jnp.zeros((X, LANES), F32)
    pad = jnp.zeros((PAD, LANES), F32)

    c_remap.wait()
    bits = X.bit_length() - 1
    code_row = remap[...]
    eye = iota((X, X), 0) == iota((X, X), 1)
    code_col = jnp.sum(jnp.where(eye, jnp.broadcast_to(code_row, (X, X)), 0), axis=1, keepdims=True)
    dest_row, dest_col = code_row >> bits, code_col >> bits
    slot_col = code_col & (X - 1)
    same = jnp.broadcast_to(dest_col, (X, X)) == jnp.broadcast_to(dest_row, (X, X))
    rank_row = jnp.sum(jnp.where(same & (iota((X, X), 0) < iota((X, X), 1)), 1, 0), axis=0, keepdims=True)
    rank_col = jnp.sum(jnp.where(same & (iota((X, X), 1) < iota((X, X), 0)), 1, 0), axis=1, keepdims=True)
    rows = 8 * GY
    row_id = iota((rows, X), 0)
    row_key = (row_id >> 3) * SLOTS + (row_id & (SLOTS - 1))
    tile_of_row = (row_key == jnp.broadcast_to(dest_row * SLOTS + rank_row, (rows, X))).astype(BF16)
    slot_of_tile = (jnp.broadcast_to(slot_col, (X, LANES)) == iota((X, LANES), 1)).astype(BF16)
    osend[...] = jnp.dot(tile_of_row, slot_of_tile, preferred_element_type=F32).reshape(GY, 8, LANES)

    pl.semaphore_wait(barrier, GY + 1)

    sends = []
    o_copies = [
        send(osend.at[peers[o]], orecv.at[gy], o_ssem.at[o], o_rsem.at[o], {"gy": peers[o]}) for o in packed_to
    ]
    sends += o_copies
    orecv[gy] = osend[gy]
    for o in whole:
        sender = side * lax.rem(my_y + side - o // side, side) + lax.rem(my_x + side - o % side, side)
        orecv[sender] = jnp.zeros((8, LANES), F32)
        frecv[sender] = jnp.zeros((3, SLOTS, LANES), F32)

    row_of_tile = jnp.broadcast_to(dest_col * 8 + rank_col, (X, rows))
    take = [(row_of_tile == iota((X, rows), 1)).astype(F32)]
    for o in whole:
        sender = side * lax.rem(my_y + side - o // side, side) + lax.rem(my_x + side - o % side, side)
        here = (dest_col == sender) & (slot_col == iota((X, X), 1))
        take.append(here.astype(F32))
    take = jnp.concatenate(take, axis=1)
    tiles[...] = jnp.zeros_like(tiles)

    c_veg.wait()
    c_table.wait()
    c_forc.wait()
    c_state.wait()
    cls = veg[...]
    nveg = table.shape[1]
    par = [jnp.full((X, LANES), table[i, 0], F32) for i in range(5)]
    for v in range(1, nveg):
        hit = cls == v
        par = [jnp.where(hit, table[i, v], par[i]) for i in range(5)]
    albedo, conduct, capacity, et_factor, decay = par
    skin = (state[0] + 0.5 * ((1.0 - albedo) * 2.0 * forc[0] + 0.5 * forc[1] + forc[2])) / 1.5
    soft = jnp.maximum(skin, 0.0) + jnp.log(1.0 + jnp.exp(-jnp.abs(skin)))
    demand = conduct * soft * (1.0 + forc[4]) * (1.0 - 0.5 * forc[3]) / (0.5 + forc[5])
    wetted = state[1] + forc[6]
    drip = jnp.maximum(wetted - capacity, 0.0)
    canopy = (wetted - drip) * capacity / (demand + capacity)
    through = drip + 0.5 * forc[6]
    draw0 = 0.5 * et_factor * demand / (1.0 + decay)
    draw1 = draw0 * decay
    landn[0] = skin
    landn[1] = canopy
    fields = jnp.concatenate([draw0, draw1, through], axis=1)
    for f, part in enumerate((draw0, draw1, through)):
        bsend[f] = part
    w_copies = [
        send(bsend, brecv.at[n], w_ssem.at[n], w_rsem.at[n], {"gy": peers[o]}) for n, o in enumerate(whole)
    ]
    sends += w_copies

    for ref in (rp, wp, ap, mp):
        for k in range(Z):
            ref[k * stride:k * stride + PAD, :] = pad
            ref[k * stride + PAD + X:(k + 1) * stride, :] = pad

    def edge_rows(k, n, value):
        usend[n, pl.ds(k, 1), :] = value[0:1]
        dsend[n, pl.ds(k, 1), :] = value[X - 1:X]

    def wet(k, turn, change=None):
        p = pc[k]
        if change is not None:
            p = p + slope[k] * change
            pc[k] = p
        s = sigmoid(p)
        r = root_conduct(s, ks[k])
        w = r * p
        (sc if turn else s0)[k] = s
        rp[layer(k), :] = r
        wp[layer(k), :] = w
        return p, s, r, w

    def near(ref, k, value):
        return (
            (ref[layer(k, -1), :] + ref[layer(k, 1), :])
            + jnp.where(first_lane, 0.0, pltpu.roll(value, 1, 1))
            + jnp.where(last_lane, 0.0, pltpu.roll(value, LANES - 1, 1))
        )

    def assemble(turn, change, k, c):
        p1, r1, kv1, qv1, diag1, res1 = c[:6]
        p, s, r, w = wet(k, turn, change)
        kv = r1 * r
        qv = kv * (p1 - p + 1.0)
        dg[block(k), :] = diag1 + kv1 + kv
        rs[block(k), :] = res1 + (qv - qv1)
        kvs[k] = kv
        sum1, sum2 = near(rp, k, r), near(wp, k, w)
        hr = 0.5 * r
        diag = 2.0 * s * (1.0 - s) + hr * sum1
        res = hr * (p * sum1 - sum2)
        if turn:
            res = res + 2.0 * (s - s0[k])
            return p, r, kv, qv, diag, res
        edge_rows(k, 0, p)
        edge_rows(k, 1, ks[k])
        acc = jnp.where(pair == k, pltpu.roll(p, 2 * k + 1, 1), c[6])
        acc = jnp.where(pair == k + HALF // 2, pltpu.roll(ks[k], HALF + 2 * k + 1, 1), acc)
        return p, r, kv, qv, diag, res, acc

    def finish(c):
        _, _, kv1, qv1, diag1, res1 = c[:6]
        dg[block(Z), :] = diag1 + kv1
        rs[block(Z), :] = res1 - qv1
        kvs[Z] = zero

    c_p.wait()
    c_k.wait()
    c = lax.fori_loop(0, Z, functools.partial(assemble, 0, None), (zero,) * 7, unroll=4)
    lsend[0] = c[6]
    finish(c)

    def halo(phase, row0, nrows):
        part = pl.ds(0, X if phase < 2 else mid)
        cs = [
            send(lsend.at[phase, part], lrecv.at[phase, 0, part], h_ssem.at[phase, 0], h_rsem.at[phase, 0], {"gy": right}),
            send(lsend.at[phase, part], lrecv.at[phase, 1, part], h_ssem.at[phase, 1], h_rsem.at[phase, 1], {"gy": left}),
            send(usend.at[pl.ds(row0, nrows)], urecv.at[pl.ds(row0, nrows)],
                 h_ssem.at[phase, 2], h_rsem.at[phase, 2], {"gx": up}),
            send(dsend.at[pl.ds(row0, nrows)], drecv.at[pl.ds(row0, nrows)],
                 h_ssem.at[phase, 3], h_rsem.at[phase, 3], {"gx": down}),
        ]
        sends.extend(cs)
        return cs

    h0 = halo(0, 0, 2)

    for c in o_copies:
        c.wait_recv()
    packed = pick_rows(orecv[...].reshape(rows, LANES)[:, :X], fields)
    for f in range(3):
        fsend[:, f, :, :] = packed[:, f * LANES:(f + 1) * LANES].reshape(GY, 8, LANES)[:, :SLOTS, :]
    f_copies = [
        send(fsend.at[peers[o]], frecv.at[gy], f_ssem.at[o], f_rsem.at[o], {"gy": peers[o]}) for o in packed_to
    ]
    sends += f_copies
    frecv[gy] = fsend[gy]

    c_a.wait()
    c_v.wait()

    def moments(k, acc):
        a = age[k]
        m = var[k] + a * a
        ap[layer(k), :] = a
        mp[layer(k), :] = m
        mom[k] = m
        edge_rows(k, 2, a)
        edge_rows(k, 3, m)
        acc = jnp.where(pair == k, pltpu.roll(a, 2 * k + 1, 1), acc)
        return jnp.where(pair == k + HALF // 2, pltpu.roll(m, HALF + 2 * k + 1, 1), acc)

    lsend[1] = lax.fori_loop(0, Z, moments, zero, unroll=4)
    h1 = halo(1, 2, 2)

    def lane_halo(phase):
        if phase >= 2:
            from_right, from_left = lrecv[phase, 1, :mid, :], lrecv[phase, 0, :mid, :]
            return jnp.concatenate(
                [
                    jnp.where(even[:mid], pltpu.roll(from_right, n - 1, 1), pltpu.roll(from_left, n % LANES + 1, 1))
                    for n in (LANES, HALF)
                ],
                axis=0,
            )
        return jnp.where(
            even, pltpu.roll(lrecv[phase, 1], LANES - 1, 1), pltpu.roll(lrecv[phase, 0], 1, 1)
        )

    for c in h0:
        c.wait_recv()
    lane_pk = lane_halo(0)
    inside = jnp.where(even, jnp.where(gy < GY - 1, 1.0, 0.0), jnp.where(gy > 0, 1.0, 0.0))
    above_in = jnp.where(gx > 0, 1.0, 0.0)
    below_in = jnp.where(gx < GX - 1, 1.0, 0.0)

    def compact_k(packed):
        return jnp.where(lane < HALF, pltpu.roll(packed, HALF, 1), 1.0)

    edge_k = (
        (compact_k(lane_pk), compact_k(lsend[0]), inside),
        (drecv[1], usend[1], above_in),
        (urecv[1], dsend[1], below_in),
    )

    def own_lanes(phase):
        if phase < 2:
            return lsend[phase]
        folded = lsend[phase, :mid, :]
        return jnp.concatenate([folded, pltpu.roll(folded, HALF, 1)], axis=0)

    def own_state(phase, n):
        return [
            (0.5 * root_conduct(sigmoid(op), ok), op)
            for (_, ok, _), op in zip(edge_k, (own_lanes(phase), usend[n], dsend[n]))
        ]

    def edge_state(phase, n, own):
        out = []
        for (hk, _, inner), hp, mine in zip(edge_k, (lane_halo(phase), drecv[n], urecv[n]), own):
            hr = root_conduct(sigmoid(hp), hk) * inner
            out.append((hr, hr * hp) + mine)
        return out

    def add_rows(ref, above, below):
        for row, value in ((0, above), (X - 1, below)):
            at = pl.ds(X + row, Z, stride=X)
            ref[at, :] = ref[at, :] + value

    def spread(k, compact):
        return jnp.where(edge, pltpu.roll(compact, LANES - 1 - 2 * k, 1), 0.0)

    def side_terms(phase, n, own):
        terms = [
            (half_r * hr, half_r * (own_p * hr - hw)) for hr, hw, half_r, own_p in edge_state(phase, n, own)
        ]
        add_rows(dg, terms[1][0], terms[2][0])
        add_rows(rs, terms[1][1], terms[2][1])
        return terms[0]

    def eliminate(k, coupling, inv, b, lanes):
        diag = dg[block(k + 1), :] + spread(k, lanes[0])
        res = rs[block(k + 1), :] + spread(k, lanes[1])
        g = coupling * inv
        b = g * b - res
        inv = 1.0 / (diag - coupling * g)
        yy[k] = b * inv
        return g, inv, b

    def from_below(lanes, k, c):
        g, inv, b = eliminate(k, kvs[k + 1], *c, lanes)
        gg[k + 1] = g
        return inv, b

    def fold_edges(k, value, acc):
        upper = pltpu.roll(value[:mid], 2 * k + 1, 1)
        lower = pltpu.roll(value[mid:], HALF + 2 * k + 1, 1)
        return jnp.where(pair[:mid] == k, upper, jnp.where(pair[:mid] == k + HALF // 2, lower, acc))

    def fold(value):
        return jnp.where(lane[:mid] < HALF, value[:mid], value[mid:])

    def update(k, n, d, acc):
        p = pc[k] + d
        pc[k] = p
        edge_rows(k, n, p)
        return fold_edges(k, p, acc)

    lanes = side_terms(0, 0, own_state(0, 0))
    c = lax.fori_loop(0, Z - 1, lambda i, c: from_below(lanes, Z - 1 - i, c), (zero, zero), unroll=4)
    inv1[...] = c[0]
    c = from_below(lanes, 0, c)
    inv0 = c[0]
    d = yy[0]
    acc = update(0, 4, d, zero[:mid])
    slope[0] = zero
    usend[6, 0:1, :] = zero[0:1]
    dsend[6, 0:1, :] = zero[0:1]

    def downward(k, c):
        d, grow, acc, acc_g = c
        g = gg[k]
        d = yy[k] + g * d
        grow = jnp.where(k > 1, g * grow, grow)
        slope[k] = grow
        edge_rows(k, 6, grow)
        acc_g = fold_edges(k, grow, acc_g)
        return d, grow, update(k, 4, d, acc), acc_g

    _, _, acc, acc_g = lax.fori_loop(1, Z, downward, (d, jnp.ones_like(zero), acc, zero[:mid]), unroll=8)
    for f in w_copies + f_copies:
        f.wait_recv()
    for f in range(3):
        tiles[f, :, :SLOTS, :] = frecv[:, f, :, :]
    given = [jnp.concatenate([tiles[f].reshape(rows, LANES) for f in range(3)], axis=1)]
    for n in range(FAR):
        given.append(jnp.concatenate([brecv[n, f] for f in range(3)], axis=1))
    got = pick_rows(take, jnp.concatenate(given, axis=0))
    ext0 = got[:, :LANES] * s0[0]
    ext1 = got[:, LANES:2 * LANES] * s0[1]
    fall = got[:, 2 * LANES:]
    limit = ks[0] * (1.0 + 2.0 * (1.0 - s0[0]))
    infil = limit * fall / (limit + fall)
    d0 = -inv0 * (ext0 - infil + gg[1] * ext1)
    d1 = gg[1] * d0 - inv1[...] * ext1

    def ends(value):
        return jnp.where(
            even,
            jnp.broadcast_to(value[:, LANES - 1:], (X, LANES)),
            jnp.broadcast_to(value[:, :1], (X, LANES)),
        )

    top = (pair[:mid] == 0) | (pair[:mid] == HALF // 2)
    lsend[2, :mid, :] = acc + acc_g * fold(ends(d1)) + jnp.where(top, fold(ends(d0)), 0.0)
    first = iota((Z, LANES), 0) == 0
    for ref, row in ((usend, 0), (dsend, X - 1)):
        d0_row, d1_row = (jnp.broadcast_to(v[row:row + 1], (Z, LANES)) for v in (d0, d1))
        ref[4] = ref[4] + ref[6] * d1_row + jnp.where(first, d0_row, 0.0)
    h2 = halo(2, 4, 1)

    pc[0] = pc[0] + d0
    c = lax.fori_loop(0, Z, functools.partial(assemble, 1, d1), (zero,) * 6, unroll=4)
    finish(c)
    rs[block(1), :] = rs[block(1), :] + (ext0 - infil)
    rs[block(2), :] = rs[block(2), :] + ext1
    own = own_state(2, 4)
    for c in h2:
        c.wait_recv()
    lanes = side_terms(2, 4, own)
    half = Z // 2

    def both_ends(i, c):
        inv_t, b_t, inv_b, b_b = c
        g, inv_t, b_t = eliminate(i, kvs[i], inv_t, b_t, lanes)
        gg[i] = g
        return (inv_t, b_t) + from_below(lanes, Z - 1 - i, (inv_b, b_b))

    inv_t, b_t, inv_b, b_b = lax.fori_loop(0, half, both_ends, (zero,) * 4, unroll=16)
    g = kvs[half] * inv_t
    d_b = (b_b + g * b_t) * inv_b / (1.0 - kvs[half] * g * inv_b)
    d_t = yy[half - 1] + g * d_b
    acc = update(half, 5, d_b, update(half - 1, 5, d_t, zero[:mid]))

    def outward(i, c):
        d_t, d_b, acc = c
        t, b = half - 1 - i, half + i
        d_t = yy[t] + gg[t + 1] * d_t
        d_b = yy[b] + gg[b] * d_b
        return d_t, d_b, update(b, 5, d_b, update(t, 5, d_t, acc))

    lsend[3, :mid, :] = lax.fori_loop(1, half, outward, (d_t, d_b, acc), unroll=15)[2]
    h3 = halo(3, 5, 1)

    def flow(t, u, u_n, m, m_n):
        t_out, t_in = jnp.maximum(t, 0.0), jnp.minimum(t, 0.0)
        return t_out * u + t_in * u_n, t_out * m + t_in * m_n

    def outflows(k, c):
        p1, r1, a1, m1, ga1, gm1, out_a1, out_m1 = c
        p, s, r, w = wet(k, 1)
        a, m = ap[layer(k), :], mp[layer(k), :]
        ga, gm = flow(r1 * r * (p1 - p + 1.0), a1, a, m1, m)
        dg[block(k), :] = out_a1 + (ga - ga1)
        rs[block(k), :] = out_m1 + (gm - gm1)
        hr = 0.5 * r
        f_a, f_m = flow(
            jnp.where(last_lane, 0.0, pltpu.roll(r, LANES - 1, 1) * p - pltpu.roll(w, LANES - 1, 1)),
            a, pltpu.roll(a, LANES - 1, 1), m, pltpu.roll(m, LANES - 1, 1),
        )
        f_a, f_m = hr * f_a, hr * f_m
        u_a, u_m = flow(rp[layer(k, -1), :] * p - wp[layer(k, -1), :], a, ap[layer(k, -1), :], m, mp[layer(k, -1), :])
        d_a, d_m = flow(rp[layer(k, 1), :] * p - wp[layer(k, 1), :], a, ap[layer(k, 1), :], m, mp[layer(k, 1), :])
        out_a = hr * (u_a + d_a) + (f_a - pltpu.roll(f_a, 1, 1))
        out_m = hr * (u_m + d_m) + (f_m - pltpu.roll(f_m, 1, 1))
        return p, r, a, m, ga, gm, out_a, out_m

    c = lax.fori_loop(0, Z, outflows, (zero,) * 8, unroll=2)
    dg[block(Z), :] = c[6] - c[4]
    rs[block(Z), :] = c[7] - c[5]
    for k, ext in ((0, ext0), (1, ext1)):
        dg[block(k + 1), :] = dg[block(k + 1), :] + ext * ap[layer(k), :]
        rs[block(k + 1), :] = rs[block(k + 1), :] + ext * mp[layer(k), :]

    own = own_state(3, 5)
    for c in h1:
        c.wait_recv()
    lane_am = lane_halo(1)
    moment_edges = (
        (lane_am, lsend[1], pltpu.roll(lane_am, HALF, 1), pltpu.roll(lsend[1], HALF, 1)),
        (drecv[2], usend[2], drecv[3], usend[3]),
        (urecv[2], dsend[2], urecv[3], dsend[3]),
    )
    for c in sends[:-len(h3)]:
        c.wait_send()
    for c in h3:
        c.wait_recv()
    terms = []
    for (hr, hw, half_r, own_p), (ha, own_a, hm, own_m) in zip(edge_state(3, 5, own), moment_edges):
        f_a, f_m = flow(hr * own_p - hw, own_a, ha, own_m, hm)
        terms.append((half_r * f_a, half_r * f_m))
    add_rows(dg, terms[1][0], terms[2][0])
    add_rows(rs, terms[1][1], terms[2][1])

    terms_out[0] = terms[0][0]
    terms_out[1] = terms[0][1]
    for c in h3:
        c.wait_send()


def finale(
    Z, X, pc, landn, dg, rs, s0, sc, age, mom, terms, p_out, a_out, v_out, land_out, av, vv, out_sem
):
    copies = []

    def store(src, dst):
        c = pltpu.make_async_copy(src, dst, out_sem.at[len(copies)])
        c.start()
        copies.append(c)

    store(pc, p_out)
    store(landn, land_out)
    lane = iota((X, LANES), 1)
    edge = (lane == 0) | (lane == LANES - 1)

    def block(k):
        return pl.ds(pl.multiple_of(k * X, 8), X)

    def spread(k, compact):
        return jnp.where(edge, pltpu.roll(compact, LANES - 1 - 2 * k, 1), 0.0)

    def ages(k, _):
        a, m = age[k], mom[k]
        out_a = dg[block(k + 1), :] + spread(k, terms[0])
        out_m = rs[block(k + 1), :] + spread(k, terms[1])
        old = 0.05 + 0.4 * s0[k]
        inv = 1.0 / (0.05 + 0.4 * sc[k])
        a2 = (old * a - 0.2 * out_a) * inv + 0.2
        av[k] = a2
        vv[k] = (old * m - 0.2 * out_m) * inv + (0.4 - a2) * a2
        return 0

    done = 0
    for end in (3 * Z // 8, 3 * Z // 4, Z):
        chunk = end - done
        lax.fori_loop(done, done + chunk, ages, 0, unroll=chunk)
        at = pl.ds(done, chunk)
        store(av.at[at], a_out.at[at])
        store(vv.at[at], v_out.at[at])
        done += chunk
    for c in copies:
        c.wait()


def shards(GX, GY, pressure, ksat, age_mean, age_var, remap, forcing, land_state, veg_class, veg_table):
    Z, X, _ = pressure.shape
    f32 = functools.partial(jax.ShapeDtypeStruct, dtype=F32)
    padded = pltpu.VMEM((Z * (X + 2 * PAD), LANES), F32)
    flat = pltpu.VMEM(((Z + 1) * X, LANES), F32)
    plain = pltpu.VMEM((Z + 1, X, LANES), F32)
    land = pltpu.VMEM(land_state.shape, F32)
    exact = pltpu.VMEM((Z, X, LANES), F32)
    dma = pltpu.SemaphoreType.DMA
    any_spec = pl.BlockSpec(memory_space=pl.ANY)
    vmem_spec = pl.BlockSpec(memory_space=pltpu.VMEM)
    inputs = (pressure, ksat, age_mean, age_var, remap.reshape(1, X), forcing, land_state, veg_class, veg_table)
    held = pl.pallas_call(
        functools.partial(kernel, Z, X, GX, GY),
        out_shape=(exact, land, flat, flat, exact, exact, exact, exact, pltpu.VMEM((2, X, LANES), F32)),
        in_specs=[any_spec] * 9,
        out_specs=(vmem_spec,) * 9,
        scratch_shapes=[padded] * 4 + [exact] + [plain] * 3 + [exact] * 2 + [pltpu.VMEM((X, LANES), F32)] + [
            pltpu.VMEM((1, X), jnp.int32),
            pltpu.VMEM(forcing.shape, F32),
            pltpu.VMEM(land_state.shape, F32),
            pltpu.VMEM(veg_class.shape, jnp.int32),
            pltpu.SMEM(veg_table.shape, F32),
            pltpu.VMEM((GY, 8, LANES), F32),
            pltpu.VMEM((GY, 8, LANES), F32),
            pltpu.VMEM((GY, 3, SLOTS, LANES), F32),
            pltpu.VMEM((GY, 3, SLOTS, LANES), F32),
            pltpu.VMEM((3, GY, 8, LANES), F32),
            pltpu.VMEM((3, X, LANES), F32),
            pltpu.VMEM((FAR, 3, X, LANES), F32),
            pltpu.VMEM((4, X, LANES), F32),
            pltpu.VMEM((4, 2, X, LANES), F32),
            pltpu.VMEM((7, Z, LANES), F32),
            pltpu.VMEM((6, Z, LANES), F32),
            pltpu.VMEM((7, Z, LANES), F32),
            pltpu.VMEM((6, Z, LANES), F32),
            dma((9,)), dma((GY,)), dma((GY,)), dma((GY,)), dma((GY,)), dma((4, 4)), dma((4, 4)), dma((FAR,)), dma((FAR,)),
        ],
        compiler_params=pltpu.CompilerParams(
            collective_id=0, has_side_effects=True, vmem_limit_bytes=24 * 1024 * 1024
        ),
    )(*(pltpu.with_memory_space_constraint(x, pltpu.HBM) for x in inputs))
    return pl.pallas_call(
        functools.partial(finale, Z, X),
        out_shape=(
            f32((Z, X, LANES)), f32((Z, X, LANES)), f32((Z, X, LANES)), f32(land_state.shape),
        ),
        in_specs=[vmem_spec] * 9,
        out_specs=(any_spec,) * 4,
        scratch_shapes=[exact, exact, dma((10,))],
        compiler_params=pltpu.CompilerParams(vmem_limit_bytes=8 * 1024 * 1024),
    )(*held)


def solution(mesh):
    field = P(None, "gx", "gy")
    return jax.shard_map(
        functools.partial(shards, mesh.shape["gx"], mesh.shape["gy"]),
        mesh=mesh,
        in_specs=(field, field, field, field, P("gx", "gy"), field, field, P("gx", "gy"), P()),
        out_specs=(field, field, field, field),
        check_vma=False,
    )
```
